32 devices in a mesh: groups: 2 (over y), param: 8 (over z, x), dp: 2 (over core).
Axes of the slice: x: 2, y: 2, z: 4, core: 2. Of those that a mesh axis runs over, the one named last changes fastest.
Arguments:
- hidden: bfloat16 [12, 128, 14336], P(('groups', 'dp'), None, 'param'), parts along dimension 0, may hold values from -6 to 6
- cotangent: bfloat16 [12, 128, 4096], P(('groups', 'dp'), None, 'param'), parts along dimension 0, may hold values from -0.5 to 0.5
- sign_flips: int32 [14336, 4096], P('param'), may hold values from -1 to 1, as said below
- offsets: int32 [8192], P('param'), may hold values from 0 to 7340031
Outputs:
- sketch: float32 [12, 8192], P(('groups', 'dp')), parts along dimension 0
The draws below stay inside these ranges and needn't reach their ends.
There are 2 independent parts, one for each index of `groups`. The reference program is written for one: setup_inputs(seed, part) draws one part's arguments, and reference() takes and returns one part's arrays. A program takes and returns all parts, laid end to end along the dimension named above; an argument that names none is the same for every part. Nothing has to cross between parts.
Inputs may be any that keep to these rules, and one draw needn't show every extreme that they name: `sign_flips`: every entry is -1 or +1.
All inputs are finite; a program needn't handle non-finite values.
Results may differ from the reference program's by a relative error of at most 0.003.
Values may be sent and summed in bfloat16 or wider, within the bound.
No kernel may reach another device: no remote copies, remote signals or barrier semaphores. Data moves between devices by JAX's collectives and lax.ppermute only.
A program may use at most 448 MiB of HBM per device.

```python
import math
import jax
import jax.numpy as jnp
from jax import lax

D = 4096
FF = 14336
K = 8192
TOK = 128
EX = 6
ROWS_DEV = 1792
KD = 1024
N_PARAM = 8


def draw_sign_flips(key, part):
    key = jax.random.fold_in(key, 11)
    coins = jax.random.randint(key, (FF, D), 0, 2)
    return (2 * coins - 1).astype(jnp.int32)


def set_ends(entries, own_key, low, largest):
    spot = [jax.random.randint(jax.random.fold_in(own_key, axis), (), 0, length) for axis, length in enumerate(entries.shape)]
    main_axis = entries.shape.index(max(entries.shape))
    neighbour = spot[:main_axis] + [(spot[main_axis] + 1) % entries.shape[main_axis]] + spot[main_axis + 1:]
    return entries.at[tuple(spot)].set(low).at[tuple(neighbour)].set(largest)


def steps_of(own_key, dims, pieces, smallest, high):
    loudness, own = 1.0, jax.random.fold_in(own_key, 6)
    for axis_at, shards_of in pieces:
        heights = jnp.exp(jax.random.uniform(jax.random.fold_in(own, axis_at), (shards_of,), jnp.float32, smallest / len(pieces), high / len(pieces)))
        loudness = loudness * jnp.repeat(heights, dims[axis_at] // shards_of).reshape([-1 if axis == axis_at else 1 for axis in range(len(dims))])
    return loudness


def noise(stream_key, shape, width, reach, cuts=(), held_as=jnp.bfloat16):
    drawn = jax.random.normal(stream_key, shape, jnp.float32) * width
    if len(cuts) > 0:
        drawn = steps_of(stream_key, shape, cuts, -0.22, 0.18) * drawn
    return jnp.clip(drawn, min=-reach, max=reach).astype(held_as)


def setup_inputs(seed: int = 0, part: int = 0) -> dict:
    key_of = jax.random.split(jax.random.key(seed), 5)
    part_keys = jax.random.split(jax.random.fold_in(key_of[4], part), 5)
    return {
        "hidden": noise(part_keys[0], (EX, TOK, FF), 1.0, 6.0, ((0, 2), (2, 8))),
        "cotangent": noise(part_keys[1], (EX, TOK, D), TOK ** -0.5, 0.5, ((0, 2), (2, 8))),
        "sign_flips": draw_sign_flips(jax.random.fold_in(key_of[4], 71), part),
        "offsets": set_ends(jax.random.randint(key_of[3], (K,), 0, ROWS_DEV * D), jax.random.fold_in(key_of[3], 1), 0, (ROWS_DEV * D) - 1).astype(jnp.int32),
    }


def walsh(signal, along):
    moved = jnp.moveaxis(signal, along, -1)
    leading = moved.shape[:-1]
    length = moved.shape[-1]
    stride = 1
    while stride < length:
        paired = moved.reshape(leading + (length // (2 * stride), 2, stride))
        upper = paired[..., 0, :]
        lower = paired[..., 1, :]
        moved = jnp.stack([upper + lower, upper - lower], axis=-2).reshape(leading + (length,))
        stride = stride * 2
    return jnp.moveaxis(moved, -1, along)

def sketch_one(paired_rows, sign_flips, offsets):
    hidden_rows, cotan_rows = paired_rows
    gradient = jnp.dot(hidden_rows.T, cotan_rows, preferred_element_type=jnp.float32).astype(jnp.bfloat16)
    flipped = (gradient * sign_flips.astype(jnp.bfloat16)).astype(jnp.float32)
    mixed = walsh(flipped, 1).reshape(N_PARAM, ROWS_DEV, D)
    mixed = walsh(mixed, 0) * (1.0 / math.sqrt(N_PARAM * D))
    shard_of = jnp.arange(K, dtype=jnp.int32) // KD
    return mixed.reshape(N_PARAM, ROWS_DEV * D)[shard_of, offsets]

def reference(hidden, cotangent, sign_flips, offsets):
    return lax.map(lambda paired_rows: sketch_one(paired_rows, sign_flips, offsets), (hidden, cotangent))
```

```python
import functools
import math

import jax
import jax.numpy as jnp
from jax import lax
from jax.experimental import pallas as pl
from jax.experimental.pallas import tpu as pltpu
from jax.sharding import PartitionSpec as P

I32, F32, BF16 = jnp.int32, jnp.float32, jnp.bfloat16
LANES = 128
HALF = 16
MIB = 2**20


def signed(word):
    return word - 2**32 if word >= 2**31 else word


def parity(bits, count):
    shift = 1
    while shift < count:
        shift *= 2
    while shift > 1:
        shift //= 2
        bits = bits ^ (bits >> shift)
    return bits & 1


def pick_tile(rows, most):
    return max(size for size in range(16, min(rows, most) + 1, 16) if rows % size == 0)


def pack_kernel(flips_ref, words_ref):
    words = None
    for tile in range(flips_ref.shape[1] // LANES):
        bit = tile // 2 + HALF * (tile % 2)
        flips = flips_ref[:, tile * LANES:(tile + 1) * LANES]
        term = (flips >> 1) & 1 if bit == 0 else flips & jnp.int32(signed(1 << bit))
        words = term if words is None else words | term
    words_ref[...] = words


def pack(sign_flips):
    rows, width = sign_flips.shape
    tile = pick_tile(rows, 256)
    return pl.pallas_call(
        pack_kernel,
        grid=(rows // tile,),
        in_specs=[pl.BlockSpec((tile, width), lambda i: (i, 0))],
        out_specs=pl.BlockSpec((tile, LANES), lambda i: (i, 0)),
        out_shape=jax.ShapeDtypeStruct((rows, LANES), I32),
        compiler_params=pltpu.CompilerParams(vmem_limit_bytes=32 * MIB),
        cost_estimate=pl.CostEstimate(flops=2 * rows * width, bytes_accessed=4 * rows * width, transcendentals=0),
        name="pack_signs",
    )(sign_flips)


def hadamard_words(column):
    length = column.shape[1]
    lane = lax.broadcasted_iota(I32, (LANES, length), 0)
    words = -parity(lane & column, 7)

    def where_bit(bit, pattern):
        return -((column >> bit) & 1) & jnp.int32(signed(pattern))

    upper = where_bit(7, 0xFFFF0000)
    for bit, pattern in ((8, 0xAAAA), (9, 0xCCCC), (10, 0xF0F0), (11, 0xFF00)):
        upper = upper ^ where_bit(bit, pattern * 0x10001)
    return words ^ upper


def gather_kernel(rows_ref, offsets_ref, words_ref, hidden_ref, signs_ref, picked_ref, held, *, length, row_shift):
    step = pl.program_id(0)
    offsets = offsets_ref[...]
    unroll = 32

    def copy_rows(group, _):
        for sub in range(unroll):
            at = group * unroll + sub
            held[pl.ds(at, 1), :] = words_ref[pl.ds(rows_ref[step * length + at], 1), :]
        return 0

    lax.fori_loop(0, length // unroll, copy_rows, 0)
    row = lax.broadcasted_iota(I32, (hidden_ref.shape[1], length), 0)
    one_hot = jnp.where(row == (offsets >> row_shift), 1.0, 0.0).astype(BF16)
    picked_ref[...] = jnp.dot(hidden_ref[...], one_hot, preferred_element_type=F32).astype(BF16)
    signs_ref[...] = held[...].T ^ hadamard_words(offsets & ((1 << row_shift) - 1))


def gather(offsets, words, hidden, width):
    count, tokens, length = offsets.shape[0], hidden.shape[0], 1024
    row_shift = width.bit_length() - 1
    return pl.pallas_call(
        functools.partial(gather_kernel, length=length, row_shift=row_shift),
        grid_spec=pltpu.PrefetchScalarGridSpec(
            num_scalar_prefetch=1,
            grid=(count // length,),
            in_specs=[
                pl.BlockSpec((1, length), lambda i, _: (0, i)),
                pl.BlockSpec(words.shape, lambda i, _: (0, 0)),
                pl.BlockSpec(hidden.shape, lambda i, _: (0, 0)),
            ],
            out_specs=[
                pl.BlockSpec((LANES, length), lambda i, _: (0, i)),
                pl.BlockSpec((tokens, length), lambda i, _: (0, i)),
            ],
            scratch_shapes=[pltpu.VMEM((length, LANES), I32)],
        ),
        out_shape=[jax.ShapeDtypeStruct((LANES, count), I32), jax.ShapeDtypeStruct((tokens, count), BF16)],
        compiler_params=pltpu.CompilerParams(vmem_limit_bytes=48 * MIB),
        cost_estimate=pl.CostEstimate(
            flops=2 * hidden.size * count, bytes_accessed=4 * LANES * count + 2 * tokens * count, transcendentals=0
        ),
        name="gather_rows",
    )(offsets >> row_shift, offsets.reshape(1, count), words, hidden)


def project_kernel(scalars, *refs, blocks, has_total, last, length, start, per_shard, parties, scale):
    cotangents = refs[:blocks]
    signs_ref, rest = refs[blocks], refs[blocks + 1:]
    total = None
    if has_total:
        total, rest = rest[0][...], rest[1:]
    words = signs_ref[...]
    halves = cotangents[0].shape[1] // (2 * LANES)
    for at in range(blocks):
        pieces = []
        for half in range(halves):
            bit = scalars[1 + at] * halves + half
            for mask in (jnp.int32(1) << bit, jnp.int32(1) << (bit + HALF)):
                pieces.append(jnp.where((words & mask) != 0, -1.0, 1.0).astype(BF16))
        term = jnp.dot(cotangents[at][...], jnp.concatenate(pieces, axis=0), preferred_element_type=F32)
        total = term if total is None else total + term
    if not last:
        rest[0][...] = total
        return
    picked_ref, out_ref = rest
    examples = out_ref.shape[0]
    position = start + pl.program_id(0) * length + lax.broadcasted_iota(I32, (1, length), 1)
    shard = position // per_shard
    sign = scale * (1 - 2 * parity(shard & scalars[0], parties.bit_length())).astype(F32)
    weighted = (total * picked_ref[...].astype(F32)).reshape(examples, -1, length)
    out_ref[...] = jnp.sum(weighted, axis=1) * sign


def project(scalars, cotangents, signs, total, picked, examples, span, per_shard, parties, scale):
    start, count = span
    tokens, depth = cotangents[0].shape
    length = 1024
    blocks = len(cotangents)
    first = start // length
    last = picked is not None
    shifted = lambda i, _: (0, i + first)
    in_specs = [pl.BlockSpec((tokens, depth), lambda i, _: (0, 0)) for _ in cotangents]
    in_specs.append(pl.BlockSpec((LANES, length), shifted))
    args = list(cotangents) + [signs]
    if total is not None:
        in_specs.append(pl.BlockSpec((tokens, length), shifted))
        args.append(total)
    if last:
        in_specs.append(pl.BlockSpec((tokens, length), shifted))
        args.append(picked)
    rows = examples if last else tokens
    return pl.pallas_call(
        functools.partial(
            project_kernel, blocks=blocks, has_total=total is not None, last=last, length=length, start=start,
            per_shard=per_shard, parties=parties, scale=scale,
        ),
        grid_spec=pltpu.PrefetchScalarGridSpec(
            num_scalar_prefetch=1,
            grid=(count // length,),
            in_specs=in_specs,
            out_specs=pl.BlockSpec((rows, length), lambda i, _: (0, i)),
        ),
        out_shape=jax.ShapeDtypeStruct((rows, count), F32),
        compiler_params=pltpu.CompilerParams(vmem_limit_bytes=56 * MIB),
        cost_estimate=pl.CostEstimate(
            flops=2 * tokens * depth * blocks * count, bytes_accessed=4 * tokens * count, transcendentals=0
        ),
        name="project_blocks",
    )(scalars, *args)


def by_xor(parties, step):
    return [(source, source ^ step) for source in range(parties)]


def exchange_offsets(offsets, own, parties):
    step = 1
    while step < parties:
        other = lax.ppermute(offsets, "param", by_xor(parties, step))
        offsets = jnp.where(
            (own & step) == 0, jnp.concatenate([offsets, other]), jnp.concatenate([other, offsets])
        )
        step *= 2
    return offsets


def sum_shards(values, parties):
    step = 1
    while step < parties:
        values = values + lax.ppermute(values, "param", by_xor(parties, step))
        step *= 2
    return values


def local(hidden, cotangent, sign_flips, offsets):
    examples, tokens, rows = hidden.shape
    width = sign_flips.shape[1]
    parties = lax.axis_size("param")
    own = lax.axis_index("param").astype(I32)
    per_shard = offsets.shape[0]
    count = per_shard * parties
    scale = 1.0 / math.sqrt(parties * width)
    flat = examples * tokens
    depth = cotangent.shape[2]
    held = cotangent.reshape(flat, depth)

    if depth % (2 * LANES) == 0 and parties % 2 == 0:
        order = list(range(0, parties, 2)) + list(range(parties - 1, 0, -2))
        forward = [(order[at], order[(at + 1) % parties]) for at in range(parties)]
        backward = [(target, source) for source, target in forward]
        place = jnp.where(own % 2 == 0, own // 2, parties - 1 - own // 2)

        def shard_at(spot):
            spot = (spot + parties) % parties
            return jnp.where(spot < parties // 2, 2 * spot, 2 * (parties - spot) - 1)

        pieces, numbers = [held], [own]
        ahead = behind = held
        for step in range(1, parties // 2):
            ahead = lax.ppermute(ahead, "param", forward)
            behind = lax.ppermute(behind, "param", backward)
            pieces += [ahead, behind]
            numbers += [shard_at(place - step), shard_at(place + step)]
        middle = flat // 2
        ahead = lax.ppermute(ahead[:middle], "param", forward)
        behind = lax.ppermute(behind[middle:], "param", backward)
        pieces.append(jnp.concatenate([ahead, behind], axis=0))
        numbers.append(shard_at(place + parties // 2))
    else:
        whole = lax.all_gather(cotangent, "param", axis=2, tiled=True).reshape(flat, width)
        span = 4 * LANES
        pieces = [whole[:, at:at + span] for at in range(0, width, span)]
        numbers = [jnp.int32(at) for at in range(len(pieces))]

    all_offsets = exchange_offsets(offsets, own, parties)
    words = pack(sign_flips)
    signs, picked = gather(all_offsets, words, hidden.reshape(flat, rows), width)

    def run(chosen, total, final, span):
        scalars = jnp.stack([own] + [numbers[at] for at in chosen])
        return project(
            scalars, [pieces[at] for at in chosen], signs, total, picked if final else None, examples, span,
            per_shard, parties, scale,
        )

    early = max(1, len(pieces) - 3)
    total = run(range(early), None, False, (0, count))
    late = range(early, len(pieces))
    half = count // 2
    parts = [sum_shards(run(late, total, True, (start, half)), parties) for start in (0, half)]
    return jnp.concatenate(parts, axis=1)


def solution(mesh):
    return jax.shard_map(
        local,
        mesh=mesh,
        in_specs=(
            P(("groups", "dp"), None, "param"),
            P(("groups", "dp"), None, "param"),
            P("param", None),
            P("param"),
        ),
        out_specs=P(("groups", "dp"), None),
        check_vma=False,
    )
```

```python
import functools
import math

import jax
import jax.numpy as jnp
from jax import lax
from jax.experimental import pallas as pl
from jax.experimental.pallas import tpu as pltpu
from jax.sharding import PartitionSpec as P

I32, F32, BF16 = jnp.int32, jnp.float32, jnp.bfloat16
LANES = 128
HALF = 16
GROUP = 8
STRIDE = 9
CHUNK = 512
MIB = 2**20
LAST_DIMS = (((1,), (1,)), ((), ()))


def signed(word):
    return word - 2**32 if word >= 2**31 else word


def parity(bits, count):
    shift = 1
    while shift < count:
        shift *= 2
    while shift > 1:
        shift //= 2
        bits = bits ^ (bits >> shift)
    return bits & 1


def table_kernel(flips_ref, hidden_ref, *refs, examples):
    table_ref = refs[-1]
    tile = flips_ref.shape[0]
    words = [None, None]
    for column in range(flips_ref.shape[1] // LANES):
        bit, part = column // 2, column % 2
        flips = flips_ref[:, column * LANES:(column + 1) * LANES]
        term = (flips >> 1) & 1 if bit == 0 else flips & jnp.int32(1 << bit)
        words[part] = term if words[part] is None else words[part] | term
    for part in range(2):
        table_ref[pl.ds(examples + part, tile, stride=GROUP), :] = words[part].astype(F32)
    tokens = hidden_ref.shape[0] // examples
    for example in range(examples):
        block = hidden_ref[example * tokens:(example + 1) * tokens, :].astype(F32).T
        table_ref[pl.ds(example, tile, stride=GROUP), :] = block[:tile]


def build_table(sign_flips, hidden, table, examples, tile, span):
    rows, width = sign_flips.shape
    first, count = span
    lanes = -(-tile // LANES) * LANES
    in_specs = [
        pl.BlockSpec((tile, width), lambda i: (i + first, 0)),
        pl.BlockSpec((hidden.shape[0], lanes), lambda i: (0, i + first)),
    ]
    args = [sign_flips, hidden]
    aliases = {}
    if table is not None:
        in_specs.append(pl.BlockSpec(memory_space=pl.ANY))
        args.append(table)
        aliases = {2: 0}
    return pl.pallas_call(
        functools.partial(table_kernel, examples=examples),
        grid=(count,),
        in_specs=in_specs,
        out_specs=pl.BlockSpec((tile * GROUP, LANES), lambda i: (i + first, 0)),
        out_shape=jax.ShapeDtypeStruct((rows * GROUP, LANES), F32),
        input_output_aliases=aliases,
        compiler_params=pltpu.CompilerParams(vmem_limit_bytes=60 * MIB),
        cost_estimate=pl.CostEstimate(
            flops=2 * tile * count * width, bytes_accessed=4 * tile * count * width, transcendentals=0
        ),
        name="build_table",
    )(*args)


def hadamard_words(column):
    length = column.shape[1]
    lane = lax.broadcasted_iota(I32, (LANES, length), 0)
    words = -parity(lane & column, 7)

    def where_bit(bit, pattern):
        return -((column >> bit) & 1) & jnp.int32(signed(pattern))

    upper = where_bit(7, 0xFFFF0000)
    for bit, pattern in ((8, 0xAAAA), (9, 0xCCCC), (10, 0xF0F0), (11, 0xFF00)):
        upper = upper ^ where_bit(bit, pattern * 0x10001)
    return words ^ upper


def sign_columns(words, bits):
    pieces = []
    for bit in bits:
        for mask in (jnp.int32(1) << bit, jnp.int32(1) << (bit + HALF)):
            pieces.append(jnp.where((words & mask) != 0, -1.0, 1.0).astype(BF16))
    return jnp.concatenate(pieces, axis=1)


def project(scalars, cotangents, words, total):
    halves = cotangents[0].shape[1] // (2 * LANES)
    for at, cotangent in enumerate(cotangents):
        first = scalars[1 + at] * halves
        columns = sign_columns(words, [first + half for half in range(halves)])
        term = lax.dot_general(cotangent[...], columns, LAST_DIMS, preferred_element_type=F32)
        total = term if total is None else total + term
    return total


def sample_kernel(
    scalars, rows_ref, offsets_ref, table_ref, *refs, blocks, examples, length, sub, first, low_mask
):
    cotangents, (signs_ref, picked_ref, total_ref, held) = refs[:blocks], refs[blocks:]
    step = pl.program_id(0)
    slot = lax.rem(step, 2)

    def copy_row(chunk, at, target):
        row = pl.multiple_of(rows_ref[first + chunk * length + at], GROUP)
        held[target, pl.ds(at * STRIDE, GROUP), :] = table_ref[pl.ds(row, GROUP), :]

    @pl.when(step == 0)
    def _():
        unroll = 32

        def copy_group(group, _):
            for at in range(unroll):
                copy_row(0, group * unroll + at, 0)
            return 0

        lax.fori_loop(0, length // unroll, copy_group, 0)

    def column(row):
        return held[slot, pl.ds(row, length, stride=STRIDE), :]

    low, high = column(examples).astype(I32), column(examples + 1).astype(I32)
    words = (low | (high << HALF)) ^ hadamard_words(offsets_ref[...] & low_mask).T
    signs_ref[...] = words
    tokens = picked_ref.shape[0] // examples
    for example in range(examples):
        picked_ref[example * tokens:(example + 1) * tokens, :] = column(example).astype(BF16).T
    following = jnp.minimum(step + 1, pl.num_programs(0) - 1)
    for start in range(0, length, sub):
        for at in range(start, start + sub):
            copy_row(following, at, 1 - slot)
        total_ref[:, start:start + sub] = project(scalars, cotangents, words[start:start + sub], None)


def sample(scalars, rows, offsets, table, cotangents, examples, span, width):
    start, count = span
    tokens, depth = cotangents[0].shape
    length = CHUNK
    first = start // length
    whole = lambda i, *_: (0, 0)
    return pl.pallas_call(
        functools.partial(
            sample_kernel, blocks=len(cotangents), examples=examples, length=length, sub=length, first=start,
            low_mask=width - 1,
        ),
        grid_spec=pltpu.PrefetchScalarGridSpec(
            num_scalar_prefetch=2,
            grid=(count // length,),
            in_specs=[pl.BlockSpec((1, length), lambda i, *_: (0, i + first)), pl.BlockSpec(table.shape, whole)]
            + [pl.BlockSpec(piece.shape, whole) for piece in cotangents],
            out_specs=[
                pl.BlockSpec((length, LANES), lambda i, *_: (i, 0)),
                pl.BlockSpec((tokens, length), lambda i, *_: (0, i)),
                pl.BlockSpec((tokens, length), lambda i, *_: (0, i)),
            ],
            scratch_shapes=[pltpu.VMEM((2, length * STRIDE, LANES), F32)],
        ),
        out_shape=[
            jax.ShapeDtypeStruct((count, LANES), I32),
            jax.ShapeDtypeStruct((tokens, count), BF16),
            jax.ShapeDtypeStruct((tokens, count), F32),
        ],
        compiler_params=pltpu.CompilerParams(vmem_limit_bytes=48 * MIB),
        cost_estimate=pl.CostEstimate(
            flops=2 * tokens * depth * len(cotangents) * count, bytes_accessed=6 * tokens * count, transcendentals=0
        ),
        name="sample_rows",
    )(scalars, rows, offsets, table, *cotangents)


def finish_kernel(
    scalars, *refs, blocks, examples, length, sub, start, per_shard, parties, scale
):
    cotangents, (signs_ref, picked_ref, total_ref, out_ref) = refs[:blocks], refs[blocks:]
    for at in range(0, length, sub):
        spot = slice(at, at + sub)
        total = project(scalars, cotangents, signs_ref[spot, :], total_ref[:, spot])
        position = start + pl.program_id(0) * length + at + lax.broadcasted_iota(I32, (1, sub), 1)
        shard = position // per_shard
        sign = scale * (1 - 2 * parity(shard & scalars[0], parties.bit_length())).astype(F32)
        weighted = (total * picked_ref[:, spot].astype(F32)).reshape(examples, -1, sub)
        out_ref[:, spot] = jnp.sum(weighted, axis=1) * sign


def finish(scalars, cotangents, signs, picked, total, examples, start, per_shard, parties, scale):
    tokens, depth = cotangents[0].shape
    count = signs.shape[0]
    sub = CHUNK // 2
    length = count // 2 if count % (2 * sub) == 0 else count
    across = lambda i, _: (0, i)
    return pl.pallas_call(
        functools.partial(
            finish_kernel, blocks=len(cotangents), examples=examples, length=length, sub=sub, start=start,
            per_shard=per_shard, parties=parties, scale=scale,
        ),
        grid_spec=pltpu.PrefetchScalarGridSpec(
            num_scalar_prefetch=1,
            grid=(count // length,),
            in_specs=[pl.BlockSpec(piece.shape, lambda i, _: (0, 0)) for piece in cotangents]
            + [
                pl.BlockSpec((length, LANES), lambda i, _: (i, 0)),
                pl.BlockSpec((tokens, length), across),
                pl.BlockSpec((tokens, length), across),
            ],
            out_specs=pl.BlockSpec((examples, length), across),
        ),
        out_shape=jax.ShapeDtypeStruct((examples, count), F32),
        compiler_params=pltpu.CompilerParams(vmem_limit_bytes=48 * MIB),
        cost_estimate=pl.CostEstimate(
            flops=2 * tokens * depth * len(cotangents) * count, bytes_accessed=6 * tokens * count, transcendentals=0
        ),
        name="finish_blocks",
    )(scalars, *cotangents, signs, picked, total)


def by_xor(parties, step):
    return [(source, source ^ step) for source in range(parties)]


def sum_shards(values, parties):
    step = 1
    while step < parties:
        values = values + lax.ppermute(values, "param", by_xor(parties, step))
        step *= 2
    return values


def local(hidden, cotangent, sign_flips, offsets):
    examples, tokens, rows = hidden.shape
    width = sign_flips.shape[1]
    parties = lax.axis_size("param")
    own = lax.axis_index("param").astype(I32)
    per_shard = offsets.shape[0]
    count = per_shard * parties
    scale = 1.0 / math.sqrt(parties * width)
    flat = examples * tokens
    depth = cotangent.shape[2]
    held = cotangent.reshape(flat, depth)

    units = hidden.reshape(flat, rows)
    if rows % LANES:
        units = jnp.pad(units, ((0, 0), (0, -rows % LANES)))
    tile = 2 * LANES if rows % (2 * LANES) == 0 else LANES if rows % LANES == 0 else rows
    tiles = rows // tile
    table, built, step = None, 0, 1
    ringed = depth % (2 * LANES) == 0 and parties % 2 == 0
    steps = parties.bit_length() - 1
    for at in range(steps):
        other = lax.ppermute(offsets, "param", by_xor(parties, step))
        until = -(-tiles * (at + 1) // steps)
        if until > built:
            table = build_table(sign_flips, units, table, examples, tile, (built, until - built))
            built = until
            table, other = lax.optimization_barrier((table, other))
        if at == 0:
            held, other = lax.optimization_barrier((held, other))
        offsets = jnp.where(
            (own & step) == 0, jnp.concatenate([offsets, other]), jnp.concatenate([other, offsets])
        )
        step *= 2

    row_shift = width.bit_length() - 1
    unit_rows = (offsets >> row_shift) * GROUP
    line = offsets.reshape(1, count)
    chunks = count // CHUNK
    bounds = [at * chunks // 3 * CHUNK for at in range(4)]
    spans = [(start, end - start) for start, end in zip(bounds, bounds[1:])]
    pieces, numbers, sampled = [held], [own], []

    def scalars(first, last):
        return jnp.stack([own] + numbers[first:last])

    def sample_next():
        return sample(
            scalars(0, len(pieces)), unit_rows, line, table, pieces, examples, spans[len(sampled)], width
        ), len(pieces)

    if ringed:
        order = list(range(0, parties, 2)) + list(range(parties - 1, 0, -2))
        forward = [(order[at], order[(at + 1) % parties]) for at in range(parties)]
        backward = [(target, source) for source, target in forward]
        place = jnp.where(own % 2 == 0, own // 2, parties - 1 - own // 2)

        def shard_at(spot):
            spot = (spot + parties) % parties
            return jnp.where(spot < parties // 2, 2 * spot, 2 * (parties - spot) - 1)

        ahead = behind = held
        for step in range(1, parties // 2):
            ahead = lax.ppermute(ahead, "param", forward)
            behind = lax.ppermute(behind, "param", backward)
            if step > 1 and len(sampled) < 3:
                sampled.append(sample_next())
                (signs, picked, total), used = sampled[-1]
                ahead, behind, signs = lax.optimization_barrier((ahead, behind, signs))
                sampled[-1] = (signs, picked, total), used
            pieces += [ahead, behind]
            numbers += [shard_at(place - step), shard_at(place + step)]
        middle = flat // 2
        ahead = lax.ppermute(ahead[:middle], "param", forward)
        behind = lax.ppermute(behind[middle:], "param", backward)
        last = jnp.concatenate([ahead, behind], axis=0)
        last_number = shard_at(place + parties // 2)
    else:
        whole = lax.all_gather(cotangent, "param", axis=2, tiled=True).reshape(flat, width)
        span = 4 * LANES
        pieces = [whole[:, at:at + span] for at in range(0, width - span, span)]
        numbers = [jnp.int32(at) for at in range(len(pieces))]
        last, last_number = whole[:, width - span:], jnp.int32(len(pieces))

    while len(sampled) < 3:
        sampled.append(sample_next())
    pieces.append(last)
    numbers.append(last_number)
    values = [
        finish(
            scalars(used, len(pieces)), pieces[used:], signs, picked, total, examples, start, per_shard, parties, scale
        )
        for ((signs, picked, total), used), (start, _) in zip(sampled, spans)
    ]
    parts = [values[0], jnp.concatenate(values[1:], axis=1)]
    return jnp.concatenate([sum_shards(part, parties) for part in parts], axis=1)


def solution(mesh):
    return jax.shard_map(
        local,
        mesh=mesh,
        in_specs=(
            P(("groups", "dp"), None, "param"),
            P(("groups", "dp"), None, "param"),
            P("param", None),
            P("param"),
        ),
        out_specs=P(("groups", "dp"), None),
        check_vma=False,
    )
```

```python
import functools
import math

import jax
import jax.numpy as jnp
from jax import lax
from jax.experimental import pallas as pl
from jax.experimental.pallas import tpu as pltpu
from jax.sharding import PartitionSpec as P

I32, F32, BF16 = jnp.int32, jnp.float32, jnp.bfloat16
LANES = 128
HALF = 16
SIGN_ROWS = 2
EARLY = ()
CHUNK = 512
MIB = 2**20
LAST_DIMS = (((1,), (1,)), ((), ()))


def signed(word):
    return word - 2**32 if word >= 2**31 else word


def parity(bits, count):
    shift = 1
    while shift < count:
        shift *= 2
    while shift > 1:
        shift //= 2
        bits = bits ^ (bits >> shift)
    return bits & 1


def table_kernel(flips_ref, hidden_ref, *refs, examples):
    table_ref = refs[-1]
    tile = flips_ref.shape[0]
    group = examples + SIGN_ROWS
    words = [None, None]
    for column in range(flips_ref.shape[1] // LANES):
        bit, part = column // 2, column % 2
        flips = flips_ref[:, column * LANES:(column + 1) * LANES]
        term = (flips >> 1) & 1 if bit == 0 else flips & jnp.int32(1 << bit)
        words[part] = term if words[part] is None else words[part] | term
    for part in range(2):
        table_ref[pl.ds(examples + part, tile, stride=group), :] = words[part].astype(F32)
    tokens = hidden_ref.shape[0] // examples
    for example in range(examples):
        block = hidden_ref[example * tokens:(example + 1) * tokens, :].astype(F32).T
        table_ref[pl.ds(example, tile, stride=group), :] = block[:tile]


def build_table(sign_flips, hidden, table, examples, tile, span):
    rows, width = sign_flips.shape
    first, count = span
    group = examples + SIGN_ROWS
    lanes = -(-tile // LANES) * LANES
    in_specs = [
        pl.BlockSpec((tile, width), lambda i: (i + first, 0)),
        pl.BlockSpec((hidden.shape[0], lanes), lambda i: (0, i + first)),
    ]
    args = [sign_flips, hidden]
    aliases = {}
    if table is not None:
        in_specs.append(pl.BlockSpec(memory_space=pl.ANY))
        args.append(table)
        aliases = {2: 0}
    return pl.pallas_call(
        functools.partial(table_kernel, examples=examples),
        grid=(count,),
        in_specs=in_specs,
        out_specs=pl.BlockSpec((tile * group, LANES), lambda i: (i + first, 0)),
        out_shape=jax.ShapeDtypeStruct((rows * group, LANES), F32),
        input_output_aliases=aliases,
        compiler_params=pltpu.CompilerParams(vmem_limit_bytes=40 * MIB),
        cost_estimate=pl.CostEstimate(
            flops=2 * tile * count * width, bytes_accessed=4 * tile * count * width, transcendentals=0
        ),
        name="build_table",
    )(*args)


def hadamard_words(column):
    length = column.shape[1]
    lane = lax.broadcasted_iota(I32, (LANES, length), 0)
    words = -parity(lane & column, 7)

    def where_bit(bit, pattern):
        return -((column >> bit) & 1) & jnp.int32(signed(pattern))

    upper = where_bit(7, 0xFFFF0000)
    for bit, pattern in ((8, 0xAAAA), (9, 0xCCCC), (10, 0xF0F0), (11, 0xFF00)):
        upper = upper ^ where_bit(bit, pattern * 0x10001)
    return words ^ upper


def sign_columns(words, bits):
    pieces = []
    for bit in bits:
        for mask in (jnp.int32(1) << bit, jnp.int32(1) << (bit + HALF)):
            pieces.append(jnp.where((words & mask) != 0, -1.0, 1.0).astype(BF16))
    return jnp.concatenate(pieces, axis=1)


def join(cotangents, joined):
    depth = cotangents[0].shape[1]
    for at, cotangent in enumerate(cotangents):
        joined[:, at * depth:(at + 1) * depth] = cotangent[...]


def project(scalars, joined, words, depth):
    halves = depth // (2 * LANES)
    bits = [scalars[1 + at] * halves + half for at in range(joined.shape[1] // depth) for half in range(halves)]
    return lax.dot_general(joined[...], sign_columns(words, bits), LAST_DIMS, preferred_element_type=F32)


def weigh(total, picked, scalars, position, examples, per_shard, parties, scale):
    shard = position // per_shard
    sign = scale * (1 - 2 * parity(shard & scalars[0], parties.bit_length())).astype(F32)
    weighted = (total * picked.astype(F32)).reshape(examples, -1, total.shape[1])
    return jnp.sum(weighted, axis=1) * sign


def sample_kernel(
    scalars, rows_ref, offsets_ref, table_ref, *refs, blocks, examples, length, first, low_mask, whole, per_shard,
    parties, scale
):
    cotangents, outs, (held, made, joined) = refs[:blocks], refs[blocks:-3], refs[-3:]
    step, steps = pl.program_id(0), pl.num_programs(0)
    group = examples + SIGN_ROWS

    def copy_row(chunk, at, slot):
        row = rows_ref[first + chunk * length + at]
        held[slot, pl.ds(at * group, group), :] = table_ref[pl.ds(row, group), :]

    def copy_chunk(chunk):
        unroll = 32
        slot = lax.rem(chunk, 3)

        def copy_group(block, _):
            for at in range(unroll):
                copy_row(chunk, block * unroll + at, slot)
            return 0

        lax.fori_loop(0, length // unroll, copy_group, 0)

    def make_words(chunk):
        slot = lax.rem(chunk, 3)
        low, high = [held[slot, pl.ds(examples + part, length, stride=group), :].astype(I32) for part in range(2)]
        start = first + jnp.minimum(chunk, steps - 1) * length
        column = offsets_ref[:, pl.ds(pl.multiple_of(start, LANES), length)] & low_mask
        made[lax.rem(chunk, 2)] = (low | (high << HALF)) ^ hadamard_words(column).T

    @pl.when(step == 0)
    def _():
        join(cotangents, joined)
        copy_chunk(0)
        copy_chunk(jnp.minimum(1, steps - 1))
        make_words(0)

    words = made[lax.rem(step, 2)]
    third = jnp.minimum(step + 2, steps - 1)
    target = lax.rem(step + 2, 3)
    for at in range(length):
        copy_row(third, at, target)
    total = project(scalars, joined, words, cotangents[0].shape[1])
    picked = [
        held[lax.rem(step, 3), pl.ds(example, length, stride=group), :].astype(BF16).T for example in range(examples)
    ]
    if whole:
        position = first + step * length + lax.broadcasted_iota(I32, (1, length), 1)
        outs[0][...] = weigh(
            total, jnp.concatenate(picked, axis=0), scalars, position, examples, per_shard, parties, scale
        )
    else:
        signs_ref, picked_ref, total_ref = outs
        total_ref[...] = total
        signs_ref[...] = words
        tokens = picked_ref.shape[0] // examples
        for example in range(examples):
            picked_ref[example * tokens:(example + 1) * tokens, :] = picked[example]
    make_words(step + 1)


def sample(scalars, rows, offsets, table, cotangents, examples, span, width, whole, per_shard, parties, scale):
    start, count = span
    tokens, depth = cotangents[0].shape
    length = CHUNK
    fixed = lambda i, *_: (0, 0)
    across = lambda i, *_: (0, i)
    if whole:
        out_specs = pl.BlockSpec((examples, length), across)
        out_shape = jax.ShapeDtypeStruct((examples, count), F32)
    else:
        out_specs = [
            pl.BlockSpec((length, LANES), lambda i, *_: (i, 0)),
            pl.BlockSpec((tokens, length), across),
            pl.BlockSpec((tokens, length), across),
        ]
        out_shape = [
            jax.ShapeDtypeStruct((count, LANES), I32),
            jax.ShapeDtypeStruct((tokens, count), BF16),
            jax.ShapeDtypeStruct((tokens, count), F32),
        ]
    return pl.pallas_call(
        functools.partial(
            sample_kernel, blocks=len(cotangents), examples=examples, length=length, first=start,
            low_mask=width - 1, whole=whole, per_shard=per_shard, parties=parties, scale=scale,
        ),
        grid_spec=pltpu.PrefetchScalarGridSpec(
            num_scalar_prefetch=2,
            grid=(count // length,),
            in_specs=[pl.BlockSpec(offsets.shape, fixed), pl.BlockSpec(table.shape, fixed)]
            + [pl.BlockSpec(piece.shape, fixed) for piece in cotangents],
            out_specs=out_specs,
            scratch_shapes=[
                pltpu.VMEM((3, length * (examples + SIGN_ROWS), LANES), F32),
                pltpu.VMEM((2, length, LANES), I32),
                pltpu.VMEM((tokens, depth * len(cotangents)), BF16),
            ],
        ),
        out_shape=out_shape,
        compiler_params=pltpu.CompilerParams(vmem_limit_bytes=40 * MIB),
        cost_estimate=pl.CostEstimate(
            flops=2 * tokens * depth * len(cotangents) * count, bytes_accessed=6 * tokens * count, transcendentals=0
        ),
        name="sample_whole" if whole else "sample_rows",
    )(scalars, rows, offsets, table, *cotangents)


def finish_kernel(
    scalars, *refs, blocks, examples, length, sub, start, per_shard, parties, scale
):
    cotangents, (signs_ref, picked_ref, total_ref, out_ref, joined) = refs[:blocks], refs[blocks:]

    @pl.when(pl.program_id(0) == 0)
    def _():
        join(cotangents, joined)

    for at in range(0, length, sub):
        spot = slice(at, at + sub)
        total = project(scalars, joined, signs_ref[spot, :], cotangents[0].shape[1]) + total_ref[:, spot]
        position = start + pl.program_id(0) * length + at + lax.broadcasted_iota(I32, (1, sub), 1)
        out_ref[:, spot] = weigh(
            total, picked_ref[:, spot], scalars, position, examples, per_shard, parties, scale
        )


def finish(scalars, cotangents, signs, picked, total, examples, start, per_shard, parties, scale):
    tokens, depth = cotangents[0].shape
    count = signs.shape[0]
    sub = CHUNK // 2
    length = count // 2 if count % (2 * sub) == 0 else count
    across = lambda i, _: (0, i)
    return pl.pallas_call(
        functools.partial(
            finish_kernel, blocks=len(cotangents), examples=examples, length=length, sub=sub, start=start,
            per_shard=per_shard, parties=parties, scale=scale,
        ),
        grid_spec=pltpu.PrefetchScalarGridSpec(
            num_scalar_prefetch=1,
            grid=(count // length,),
            in_specs=[pl.BlockSpec(piece.shape, lambda i, _: (0, 0)) for piece in cotangents]
            + [
                pl.BlockSpec((length, LANES), lambda i, _: (i, 0)),
                pl.BlockSpec((tokens, length), across),
                pl.BlockSpec((tokens, length), across),
            ],
            out_specs=pl.BlockSpec((examples, length), across),
            scratch_shapes=[pltpu.VMEM((tokens, depth * len(cotangents)), BF16)],
        ),
        out_shape=jax.ShapeDtypeStruct((examples, count), F32),
        compiler_params=pltpu.CompilerParams(vmem_limit_bytes=48 * MIB),
        cost_estimate=pl.CostEstimate(
            flops=2 * tokens * depth * len(cotangents) * count, bytes_accessed=6 * tokens * count, transcendentals=0
        ),
        name="finish_blocks",
    )(scalars, *cotangents, signs, picked, total)


def by_xor(parties, step):
    return [(source, source ^ step) for source in range(parties)]


def sum_shards(values, parties):
    step = 1
    while step < parties:
        values = values + lax.ppermute(values, "param", by_xor(parties, step))
        step *= 2
    return values


def local(hidden, cotangent, sign_flips, offsets):
    examples, tokens, rows = hidden.shape
    width = sign_flips.shape[1]
    parties = lax.axis_size("param")
    own = lax.axis_index("param").astype(I32)
    per_shard = offsets.shape[0]
    count = per_shard * parties
    scale = 1.0 / math.sqrt(parties * width)
    flat = examples * tokens
    depth = cotangent.shape[2]
    held = cotangent.reshape(flat, depth)

    ringed = depth % (2 * LANES) == 0 and parties % 2 == 0
    pieces, numbers = [held], [own]
    if ringed:
        order = list(range(0, parties, 2)) + list(range(parties - 1, 0, -2))
        forward = [(order[at], order[(at + 1) % parties]) for at in range(parties)]
        backward = [(target, source) for source, target in forward]
        place = jnp.where(own % 2 == 0, own // 2, parties - 1 - own // 2)

        def shard_at(spot):
            spot = (spot + parties) % parties
            return jnp.where(spot < parties // 2, 2 * spot, 2 * (parties - spot) - 1)

        def pass_on(ahead, behind):
            return lax.ppermute(ahead, "param", forward), lax.ppermute(behind, "param", backward)

    units = hidden.reshape(flat, rows)
    if rows % LANES:
        units = jnp.pad(units, ((0, 0), (0, -rows % LANES)))
    tile = 2 * LANES if rows % (2 * LANES) == 0 else LANES if rows % LANES == 0 else rows
    tiles = rows // tile
    table, built, step = None, 0, 1
    steps = parties.bit_length() - 1
    for at in range(steps):
        other = lax.ppermute(offsets, "param", by_xor(parties, step))
        until = tiles - (tiles - 1) * (steps - 1 - at) // max(steps - 1, 1)
        if until > built:
            table = build_table(sign_flips, units, table, examples, tile, (built, until - built))
            built = until
            table, other = lax.optimization_barrier((table, other))
        if ringed and at == 0:
            held, other = lax.optimization_barrier((held, other))
            ahead, behind = pass_on(held, held)
        if ringed and at == 1:
            table, ahead, behind = lax.optimization_barrier((table, ahead, behind))
        offsets = jnp.where(
            (own & step) == 0, jnp.concatenate([offsets, other]), jnp.concatenate([other, offsets])
        )
        step *= 2

    row_shift = width.bit_length() - 1
    unit_rows = (offsets >> row_shift) * (examples + SIGN_ROWS)
    line = offsets.reshape(1, count)
    eighth = count // 8
    sizes = [part * eighth for part in EARLY] if ringed else []
    sizes.append(count - sum(sizes))
    spans = [(sum(sizes[:at]), size) for at, size in enumerate(sizes)]
    sampled = []

    def scalars(first, last):
        return jnp.stack([own] + numbers[first:last])

    def sample_next(whole):
        return sample(
            scalars(0, len(pieces)), unit_rows, line, table, pieces, examples, spans[len(sampled)], width, whole,
            per_shard, parties, scale,
        )

    if ringed:
        for step in range(1, parties // 2):
            pieces += [ahead, behind]
            numbers += [shard_at(place - step), shard_at(place + step)]
            if step + 1 < parties // 2:
                ahead, behind = pass_on(ahead, behind)
            else:
                middle = flat // 2
                ahead, behind = pass_on(ahead[:middle], behind[middle:])
            if step > 1 and len(sampled) < len(EARLY):
                signs, picked, total = sample_next(False)
                ahead, behind, signs = lax.optimization_barrier((ahead, behind, signs))
                sampled.append((signs, picked, total, len(pieces)))
        pieces.append(jnp.concatenate([ahead, behind], axis=0))
        numbers.append(shard_at(place + parties // 2))
    else:
        gathered = lax.all_gather(cotangent, "param", axis=2, tiled=True).reshape(flat, width)
        span = 4 * LANES
        pieces = [gathered[:, at:at + span] for at in range(0, width, span)]
        numbers = [jnp.int32(at) for at in range(len(pieces))]
    whole = sample_next(True)
    parts = [whole]
    if sampled:
        parts = [
            finish(
                scalars(used, len(pieces)), pieces[used:], signs, picked, total, examples, start, per_shard, parties,
                scale,
            )
            for (signs, picked, total, used), (start, _) in zip(sampled, spans)
        ]
        parts = [jnp.concatenate(parts, axis=1), whole]
    return jnp.concatenate([sum_shards(part, parties) for part in parts], axis=1)


def solution(mesh):
    return jax.shard_map(
        local,
        mesh=mesh,
        in_specs=(
            P(("groups", "dp"), None, "param"),
            P(("groups", "dp"), None, "param"),
            P("param", None),
            P("param"),
        ),
        out_specs=P(("groups", "dp"), None),
        check_vma=False,
    )
```

```python
import functools
import math

import jax
import jax.numpy as jnp
from jax import lax
from jax.experimental import pallas as pl
from jax.experimental.pallas import tpu as pltpu
from jax.sharding import PartitionSpec as P

I32, F32, BF16 = jnp.int32, jnp.float32, jnp.bfloat16
LANES = 128
HALF = 16
SIGN_ROWS = 2
EARLY = ()
CHUNK = 512
MIB = 2**20
LAST_DIMS = (((1,), (1,)), ((), ()))


def signed(word):
    return word - 2**32 if word >= 2**31 else word


def parity(bits, count):
    shift = 1
    while shift < count:
        shift *= 2
    while shift > 1:
        shift //= 2
        bits = bits ^ (bits >> shift)
    return bits & 1


def table_kernel(flips_ref, hidden_ref, *refs, examples):
    table_ref = refs[-1]
    tile = flips_ref.shape[0]
    group = examples + SIGN_ROWS
    words = [None, None]
    for column in range(flips_ref.shape[1] // LANES):
        bit, part = column // 2, column % 2
        flips = flips_ref[:, column * LANES:(column + 1) * LANES]
        term = (flips >> 1) & 1 if bit == 0 else flips & jnp.int32(1 << bit)
        words[part] = term if words[part] is None else words[part] | term
    for part in range(2):
        table_ref[pl.ds(examples + part, tile, stride=group), :] = words[part].astype(F32)
    tokens = hidden_ref.shape[0] // examples
    for example in range(examples):
        block = hidden_ref[example * tokens:(example + 1) * tokens, :].astype(F32).T
        table_ref[pl.ds(example, tile, stride=group), :] = block[:tile]


def build_table(sign_flips, hidden, table, examples, tile, span):
    rows, width = sign_flips.shape
    first, count = span
    group = examples + SIGN_ROWS
    lanes = -(-tile // LANES) * LANES
    in_specs = [
        pl.BlockSpec((tile, width), lambda i: (i + first, 0)),
        pl.BlockSpec((hidden.shape[0], lanes), lambda i: (0, i + first)),
    ]
    args = [sign_flips, hidden]
    aliases = {}
    if table is not None:
        in_specs.append(pl.BlockSpec(memory_space=pl.ANY))
        args.append(table)
        aliases = {2: 0}
    return pl.pallas_call(
        functools.partial(table_kernel, examples=examples),
        grid=(count,),
        in_specs=in_specs,
        out_specs=pl.BlockSpec((tile * group, LANES), lambda i: (i + first, 0)),
        out_shape=jax.ShapeDtypeStruct((rows * group, LANES), F32),
        input_output_aliases=aliases,
        compiler_params=pltpu.CompilerParams(vmem_limit_bytes=60 * MIB),
        cost_estimate=pl.CostEstimate(
            flops=2 * tile * count * width, bytes_accessed=4 * tile * count * width, transcendentals=0
        ),
        name="build_table",
    )(*args)


def hadamard_words(column):
    length = column.shape[1]
    lane = lax.broadcasted_iota(I32, (LANES, length), 0)
    words = -parity(lane & column, 7)

    def where_bit(bit, pattern):
        return -((column >> bit) & 1) & jnp.int32(signed(pattern))

    upper = where_bit(7, 0xFFFF0000)
    for bit, pattern in ((8, 0xAAAA), (9, 0xCCCC), (10, 0xF0F0), (11, 0xFF00)):
        upper = upper ^ where_bit(bit, pattern * 0x10001)
    return words ^ upper


def sign_columns(words, bits):
    pieces = []
    for bit in bits:
        for mask in (jnp.int32(1) << bit, jnp.int32(1) << (bit + HALF)):
            pieces.append(jnp.where((words & mask) != 0, -1.0, 1.0).astype(BF16))
    return jnp.concatenate(pieces, axis=1)


def join(cotangents, joined):
    depth = cotangents[0].shape[1]
    for at, cotangent in enumerate(cotangents):
        joined[:, at * depth:(at + 1) * depth] = cotangent[...]


def project(scalars, joined, words, depth):
    halves = depth // (2 * LANES)
    bits = [scalars[1 + at] * halves + half for at in range(joined.shape[1] // depth) for half in range(halves)]
    return lax.dot_general(joined[...], sign_columns(words, bits), LAST_DIMS, preferred_element_type=F32)


def weigh(total, picked, scalars, position, examples, per_shard, parties, scale):
    shard = position // per_shard
    sign = scale * (1 - 2 * parity(shard & scalars[0], parties.bit_length())).astype(F32)
    weighted = (total * picked.astype(F32)).reshape(examples, -1, total.shape[1])
    return jnp.sum(weighted, axis=1) * sign


def sample_kernel(
    scalars, rows_ref, offsets_ref, table_ref, *refs, blocks, examples, length, first, low_mask, whole, per_shard,
    parties, scale
):
    cotangents, outs, (held, made, joined) = refs[:blocks], refs[blocks:-3], refs[-3:]
    step, steps = pl.program_id(0), pl.num_programs(0)
    group = examples + SIGN_ROWS

    def copy_row(chunk, at, slot):
        row = rows_ref[first + chunk * length + at]
        held[slot, pl.ds(at * group, group), :] = table_ref[pl.ds(row, group), :]

    def copy_chunk(chunk):
        unroll = 32
        slot = lax.rem(chunk, 3)

        def copy_group(block, _):
            for at in range(unroll):
                copy_row(chunk, block * unroll + at, slot)
            return 0

        lax.fori_loop(0, length // unroll, copy_group, 0)

    def make_words(chunk):
        slot = lax.rem(chunk, 3)
        low, high = [held[slot, pl.ds(examples + part, length, stride=group), :].astype(I32) for part in range(2)]
        start = first + jnp.minimum(chunk, steps - 1) * length
        column = offsets_ref[:, pl.ds(pl.multiple_of(start, LANES), length)] & low_mask
        made[lax.rem(chunk, 2)] = (low | (high << HALF)) ^ hadamard_words(column).T

    @pl.when(step == 0)
    def _():
        join(cotangents, joined)
        copy_chunk(0)
        copy_chunk(jnp.minimum(1, steps - 1))
        make_words(0)

    words = made[lax.rem(step, 2)]
    third = jnp.minimum(step + 2, steps - 1)
    target = lax.rem(step + 2, 3)
    for at in range(length):
        copy_row(third, at, target)
    total = project(scalars, joined, words, cotangents[0].shape[1])
    picked = [
        held[lax.rem(step, 3), pl.ds(example, length, stride=group), :].astype(BF16).T for example in range(examples)
    ]
    if whole:
        position = first + step * length + lax.broadcasted_iota(I32, (1, length), 1)
        outs[0][...] = weigh(
            total, jnp.concatenate(picked, axis=0), scalars, position, examples, per_shard, parties, scale
        )
    else:
        signs_ref, picked_ref, total_ref = outs
        total_ref[...] = total
        signs_ref[...] = words
        tokens = picked_ref.shape[0] // examples
        for example in range(examples):
            picked_ref[example * tokens:(example + 1) * tokens, :] = picked[example]
    make_words(step + 1)


def sample(scalars, rows, offsets, table, cotangents, examples, span, width, whole, per_shard, parties, scale):
    start, count = span
    tokens, depth = cotangents[0].shape
    length = CHUNK
    fixed = lambda i, *_: (0, 0)
    across = lambda i, *_: (0, i)
    if whole:
        out_specs = pl.BlockSpec((examples, length), across)
        out_shape = jax.ShapeDtypeStruct((examples, count), F32)
    else:
        out_specs = [
            pl.BlockSpec((length, LANES), lambda i, *_: (i, 0)),
            pl.BlockSpec((tokens, length), across),
            pl.BlockSpec((tokens, length), across),
        ]
        out_shape = [
            jax.ShapeDtypeStruct((count, LANES), I32),
            jax.ShapeDtypeStruct((tokens, count), BF16),
            jax.ShapeDtypeStruct((tokens, count), F32),
        ]
    return pl.pallas_call(
        functools.partial(
            sample_kernel, blocks=len(cotangents), examples=examples, length=length, first=start,
            low_mask=width - 1, whole=whole, per_shard=per_shard, parties=parties, scale=scale,
        ),
        grid_spec=pltpu.PrefetchScalarGridSpec(
            num_scalar_prefetch=2,
            grid=(count // length,),
            in_specs=[pl.BlockSpec(offsets.shape, fixed), pl.BlockSpec(table.shape, fixed)]
            + [pl.BlockSpec(piece.shape, fixed) for piece in cotangents],
            out_specs=out_specs,
            scratch_shapes=[
                pltpu.VMEM((3, length * (examples + SIGN_ROWS), LANES), F32),
                pltpu.VMEM((2, length, LANES), I32),
                pltpu.VMEM((tokens, depth * len(cotangents)), BF16),
            ],
        ),
        out_shape=out_shape,
        compiler_params=pltpu.CompilerParams(vmem_limit_bytes=56 * MIB),
        cost_estimate=pl.CostEstimate(
            flops=2 * tokens * depth * len(cotangents) * count, bytes_accessed=6 * tokens * count, transcendentals=0
        ),
        name="sample_whole" if whole else "sample_rows",
    )(scalars, rows, offsets, table, *cotangents)


def finish_kernel(
    scalars, *refs, blocks, examples, length, sub, start, per_shard, parties, scale
):
    cotangents, (signs_ref, picked_ref, total_ref, out_ref, joined) = refs[:blocks], refs[blocks:]

    @pl.when(pl.program_id(0) == 0)
    def _():
        join(cotangents, joined)

    for at in range(0, length, sub):
        spot = slice(at, at + sub)
        total = project(scalars, joined, signs_ref[spot, :], cotangents[0].shape[1]) + total_ref[:, spot]
        position = start + pl.program_id(0) * length + at + lax.broadcasted_iota(I32, (1, sub), 1)
        out_ref[:, spot] = weigh(
            total, picked_ref[:, spot], scalars, position, examples, per_shard, parties, scale
        )


def finish(scalars, cotangents, signs, picked, total, examples, start, per_shard, parties, scale):
    tokens, depth = cotangents[0].shape
    count = signs.shape[0]
    sub = CHUNK // 2
    length = count // 2 if count % (2 * sub) == 0 else count
    across = lambda i, _: (0, i)
    return pl.pallas_call(
        functools.partial(
            finish_kernel, blocks=len(cotangents), examples=examples, length=length, sub=sub, start=start,
            per_shard=per_shard, parties=parties, scale=scale,
        ),
        grid_spec=pltpu.PrefetchScalarGridSpec(
            num_scalar_prefetch=1,
            grid=(count // length,),
            in_specs=[pl.BlockSpec(piece.shape, lambda i, _: (0, 0)) for piece in cotangents]
            + [
                pl.BlockSpec((length, LANES), lambda i, _: (i, 0)),
                pl.BlockSpec((tokens, length), across),
                pl.BlockSpec((tokens, length), across),
            ],
            out_specs=pl.BlockSpec((examples, length), across),
            scratch_shapes=[pltpu.VMEM((tokens, depth * len(cotangents)), BF16)],
        ),
        out_shape=jax.ShapeDtypeStruct((examples, count), F32),
        compiler_params=pltpu.CompilerParams(vmem_limit_bytes=48 * MIB),
        cost_estimate=pl.CostEstimate(
            flops=2 * tokens * depth * len(cotangents) * count, bytes_accessed=6 * tokens * count, transcendentals=0
        ),
        name="finish_blocks",
    )(scalars, *cotangents, signs, picked, total)


def by_xor(parties, step):
    return [(source, source ^ step) for source in range(parties)]


def sum_shards(values, parties):
    step = 1
    while step < parties:
        values = values + lax.ppermute(values, "param", by_xor(parties, step))
        step *= 2
    return values


def local(hidden, cotangent, sign_flips, offsets):
    examples, tokens, rows = hidden.shape
    width = sign_flips.shape[1]
    parties = lax.axis_size("param")
    own = lax.axis_index("param").astype(I32)
    per_shard = offsets.shape[0]
    count = per_shard * parties
    scale = 1.0 / math.sqrt(parties * width)
    flat = examples * tokens
    depth = cotangent.shape[2]
    held = cotangent.reshape(flat, depth)

    ringed = depth % (2 * LANES) == 0 and parties % 2 == 0
    pieces, numbers = [held], [own]
    if ringed:
        order = list(range(0, parties, 2)) + list(range(parties - 1, 0, -2))
        forward = [(order[at], order[(at + 1) % parties]) for at in range(parties)]
        backward = [(target, source) for source, target in forward]
        place = jnp.where(own % 2 == 0, own // 2, parties - 1 - own // 2)

        def shard_at(spot):
            spot = (spot + parties) % parties
            return jnp.where(spot < parties // 2, 2 * spot, 2 * (parties - spot) - 1)

        def pass_on(ahead, behind):
            return lax.ppermute(ahead, "param", forward), lax.ppermute(behind, "param", backward)

        ahead, behind = pass_on(held, held)

    units = hidden.reshape(flat, rows)
    if rows % LANES:
        units = jnp.pad(units, ((0, 0), (0, -rows % LANES)))
    tile = 2 * LANES if rows % (2 * LANES) == 0 else LANES if rows % LANES == 0 else rows
    tiles = rows // tile
    table, built, step = None, 0, 1
    steps = parties.bit_length() - 1
    for at in range(steps):
        other = lax.ppermute(offsets, "param", by_xor(parties, step))
        until = -(-tiles * (at + 1) // steps)
        if until > built:
            table = build_table(sign_flips, units, table, examples, tile, (built, until - built))
            built = until
            table, other = lax.optimization_barrier((table, other))
        if ringed and at == 1:
            table, ahead, behind = lax.optimization_barrier((table, ahead, behind))
        offsets = jnp.where(
            (own & step) == 0, jnp.concatenate([offsets, other]), jnp.concatenate([other, offsets])
        )
        step *= 2

    row_shift = width.bit_length() - 1
    unit_rows = (offsets >> row_shift) * (examples + SIGN_ROWS)
    line = offsets.reshape(1, count)
    eighth = count // 8
    sizes = [part * eighth for part in EARLY] if ringed else []
    sizes.append(count - sum(sizes))
    spans = [(sum(sizes[:at]), size) for at, size in enumerate(sizes)]
    sampled = []

    def scalars(first, last):
        return jnp.stack([own] + numbers[first:last])

    def sample_next(whole):
        return sample(
            scalars(0, len(pieces)), unit_rows, line, table, pieces, examples, spans[len(sampled)], width, whole,
            per_shard, parties, scale,
        )

    if ringed:
        for step in range(1, parties // 2):
            pieces += [ahead, behind]
            numbers += [shard_at(place - step), shard_at(place + step)]
            if step == 2:
                ahead, behind, table = lax.optimization_barrier((ahead, behind, table))
            if step + 1 < parties // 2:
                ahead, behind = pass_on(ahead, behind)
            else:
                middle = flat // 2
                ahead, behind = pass_on(ahead[:middle], behind[middle:])
            if step > 1 and len(sampled) < len(EARLY):
                signs, picked, total = sample_next(False)
                ahead, behind, signs = lax.optimization_barrier((ahead, behind, signs))
                sampled.append((signs, picked, total, len(pieces)))
        pieces.append(jnp.concatenate([ahead, behind], axis=0))
        numbers.append(shard_at(place + parties // 2))
    else:
        gathered = lax.all_gather(cotangent, "param", axis=2, tiled=True).reshape(flat, width)
        span = 4 * LANES
        pieces = [gathered[:, at:at + span] for at in range(0, width, span)]
        numbers = [jnp.int32(at) for at in range(len(pieces))]
    whole = sample_next(True)
    parts = [whole[:, :count // 2], whole[:, count // 2:]]
    if sampled:
        parts = [
            finish(
                scalars(used, len(pieces)), pieces[used:], signs, picked, total, examples, start, per_shard, parties,
                scale,
            )
            for (signs, picked, total, used), (start, _) in zip(sampled, spans)
        ]
        parts = [jnp.concatenate(parts, axis=1), whole]
    return jnp.concatenate([sum_shards(part, parties) for part in parts], axis=1)


def solution(mesh):
    return jax.shard_map(
        local,
        mesh=mesh,
        in_specs=(
            P(("groups", "dp"), None, "param"),
            P(("groups", "dp"), None, "param"),
            P("param", None),
            P("param"),
        ),
        out_specs=P(("groups", "dp"), None),
        check_vma=False,
    )
```

```python
import functools
import math

import jax
import jax.numpy as jnp
from jax import lax
from jax.experimental import pallas as pl
from jax.experimental.pallas import tpu as pltpu
from jax.sharding import PartitionSpec as P

I32, F32, BF16 = jnp.int32, jnp.float32, jnp.bfloat16
LANES = 128
HALF = 16
SIGN_ROWS = 2
EARLY = ()
CHUNK = 512
MIB = 2**20
LAST_DIMS = (((1,), (1,)), ((), ()))


def signed(word):
    return word - 2**32 if word >= 2**31 else word


def parity(bits, count):
    shift = 1
    while shift < count:
        shift *= 2
    while shift > 1:
        shift //= 2
        bits = bits ^ (bits >> shift)
    return bits & 1


def table_kernel(flips_ref, hidden_ref, *refs, examples):
    table_ref = refs[-1]
    tile = flips_ref.shape[0]
    group = examples + SIGN_ROWS
    words = [None, None]
    for column in range(flips_ref.shape[1] // LANES):
        bit, part = column // 2, column % 2
        flips = flips_ref[:, column * LANES:(column + 1) * LANES]
        term = (flips >> 1) & 1 if bit == 0 else flips & jnp.int32(1 << bit)
        words[part] = term if words[part] is None else words[part] | term
    for part in range(2):
        table_ref[pl.ds(examples + part, tile, stride=group), :] = words[part].astype(F32)
    tokens = hidden_ref.shape[0] // examples
    for example in range(examples):
        block = hidden_ref[example * tokens:(example + 1) * tokens, :].astype(F32).T
        table_ref[pl.ds(example, tile, stride=group), :] = block[:tile]


def build_table(sign_flips, hidden, table, examples, tile, span):
    rows, width = sign_flips.shape
    first, count = span
    group = examples + SIGN_ROWS
    lanes = -(-tile // LANES) * LANES
    in_specs = [
        pl.BlockSpec((tile, width), lambda i: (i + first, 0)),
        pl.BlockSpec((hidden.shape[0], lanes), lambda i: (0, i + first)),
    ]
    args = [sign_flips, hidden]
    aliases = {}
    if table is not None:
        in_specs.append(pl.BlockSpec(memory_space=pl.ANY))
        args.append(table)
        aliases = {2: 0}
    return pl.pallas_call(
        functools.partial(table_kernel, examples=examples),
        grid=(count,),
        in_specs=in_specs,
        out_specs=pl.BlockSpec((tile * group, LANES), lambda i: (i + first, 0)),
        out_shape=jax.ShapeDtypeStruct((rows * group, LANES), F32),
        input_output_aliases=aliases,
        compiler_params=pltpu.CompilerParams(vmem_limit_bytes=60 * MIB),
        cost_estimate=pl.CostEstimate(
            flops=2 * tile * count * width, bytes_accessed=4 * tile * count * width, transcendentals=0
        ),
        name="build_table",
    )(*args)


def hadamard_words(column):
    length = column.shape[1]
    lane = lax.broadcasted_iota(I32, (LANES, length), 0)
    words = -parity(lane & column, 7)

    def where_bit(bit, pattern):
        return -((column >> bit) & 1) & jnp.int32(signed(pattern))

    upper = where_bit(7, 0xFFFF0000)
    for bit, pattern in ((8, 0xAAAA), (9, 0xCCCC), (10, 0xF0F0), (11, 0xFF00)):
        upper = upper ^ where_bit(bit, pattern * 0x10001)
    return words ^ upper


def sign_columns(words, bits):
    pieces = []
    for bit in bits:
        for mask in (jnp.int32(1) << bit, jnp.int32(1) << (bit + HALF)):
            pieces.append(jnp.where((words & mask) != 0, -1.0, 1.0).astype(BF16))
    return jnp.concatenate(pieces, axis=1)


def join(cotangents, joined):
    depth = cotangents[0].shape[1]
    for at, cotangent in enumerate(cotangents):
        joined[:, at * depth:(at + 1) * depth] = cotangent[...]


def project(scalars, joined, words, depth):
    halves = depth // (2 * LANES)
    bits = [scalars[1 + at] * halves + half for at in range(joined.shape[1] // depth) for half in range(halves)]
    return lax.dot_general(joined[...], sign_columns(words, bits), LAST_DIMS, preferred_element_type=F32)


def weigh(total, picked, scalars, position, examples, per_shard, parties, scale):
    shard = position // per_shard
    sign = scale * (1 - 2 * parity(shard & scalars[0], parties.bit_length())).astype(F32)
    weighted = (total * picked.astype(F32)).reshape(examples, -1, total.shape[1])
    return jnp.sum(weighted, axis=1) * sign


def sample_kernel(
    scalars, rows_ref, offsets_ref, table_ref, *refs, blocks, examples, length, first, low_mask, whole, per_shard,
    parties, scale
):
    cotangents, outs, (held, made, joined) = refs[:blocks], refs[blocks:-3], refs[-3:]
    step, steps = pl.program_id(0), pl.num_programs(0)
    group = examples + SIGN_ROWS

    def copy_row(chunk, at, slot):
        row = rows_ref[first + chunk * length + at]
        held[slot, pl.ds(at * group, group), :] = table_ref[pl.ds(row, group), :]

    def copy_chunk(chunk):
        unroll = 32
        slot = lax.rem(chunk, 3)

        def copy_group(block, _):
            for at in range(unroll):
                copy_row(chunk, block * unroll + at, slot)
            return 0

        lax.fori_loop(0, length // unroll, copy_group, 0)

    def make_words(chunk):
        slot = lax.rem(chunk, 3)
        low, high = [held[slot, pl.ds(examples + part, length, stride=group), :].astype(I32) for part in range(2)]
        start = first + jnp.minimum(chunk, steps - 1) * length
        column = offsets_ref[:, pl.ds(pl.multiple_of(start, LANES), length)] & low_mask
        made[lax.rem(chunk, 2)] = (low | (high << HALF)) ^ hadamard_words(column).T

    @pl.when(step == 0)
    def _():
        join(cotangents, joined)
        copy_chunk(0)
        copy_chunk(jnp.minimum(1, steps - 1))
        make_words(0)

    words = made[lax.rem(step, 2)]
    third = jnp.minimum(step + 2, steps - 1)
    target = lax.rem(step + 2, 3)
    for at in range(length):
        copy_row(third, at, target)
    total = project(scalars, joined, words, cotangents[0].shape[1])
    picked = [
        held[lax.rem(step, 3), pl.ds(example, length, stride=group), :].astype(BF16).T for example in range(examples)
    ]
    if whole:
        position = first + step * length + lax.broadcasted_iota(I32, (1, length), 1)
        outs[0][...] = weigh(
            total, jnp.concatenate(picked, axis=0), scalars, position, examples, per_shard, parties, scale
        )
    else:
        signs_ref, picked_ref, total_ref = outs
        total_ref[...] = total
        signs_ref[...] = words
        tokens = picked_ref.shape[0] // examples
        for example in range(examples):
            picked_ref[example * tokens:(example + 1) * tokens, :] = picked[example]
    make_words(step + 1)


def sample(scalars, rows, offsets, table, cotangents, examples, span, width, whole, per_shard, parties, scale):
    start, count = span
    tokens, depth = cotangents[0].shape
    length = CHUNK
    fixed = lambda i, *_: (0, 0)
    across = lambda i, *_: (0, i)
    if whole:
        out_specs = pl.BlockSpec((examples, length), across)
        out_shape = jax.ShapeDtypeStruct((examples, count), F32)
    else:
        out_specs = [
            pl.BlockSpec((length, LANES), lambda i, *_: (i, 0)),
            pl.BlockSpec((tokens, length), across),
            pl.BlockSpec((tokens, length), across),
        ]
        out_shape = [
            jax.ShapeDtypeStruct((count, LANES), I32),
            jax.ShapeDtypeStruct((tokens, count), BF16),
            jax.ShapeDtypeStruct((tokens, count), F32),
        ]
    return pl.pallas_call(
        functools.partial(
            sample_kernel, blocks=len(cotangents), examples=examples, length=length, first=start,
            low_mask=width - 1, whole=whole, per_shard=per_shard, parties=parties, scale=scale,
        ),
        grid_spec=pltpu.PrefetchScalarGridSpec(
            num_scalar_prefetch=2,
            grid=(count // length,),
            in_specs=[pl.BlockSpec(offsets.shape, fixed), pl.BlockSpec(table.shape, fixed)]
            + [pl.BlockSpec(piece.shape, fixed) for piece in cotangents],
            out_specs=out_specs,
            scratch_shapes=[
                pltpu.VMEM((3, length * (examples + SIGN_ROWS), LANES), F32),
                pltpu.VMEM((2, length, LANES), I32),
                pltpu.VMEM((tokens, depth * len(cotangents)), BF16),
            ],
        ),
        out_shape=out_shape,
        compiler_params=pltpu.CompilerParams(vmem_limit_bytes=44 * MIB),
        cost_estimate=pl.CostEstimate(
            flops=2 * tokens * depth * len(cotangents) * count, bytes_accessed=6 * tokens * count, transcendentals=0
        ),
        name="sample_whole" if whole else "sample_rows",
    )(scalars, rows, offsets, table, *cotangents)


def finish_kernel(
    scalars, *refs, blocks, examples, length, sub, start, per_shard, parties, scale
):
    cotangents, (signs_ref, picked_ref, total_ref, out_ref, joined) = refs[:blocks], refs[blocks:]

    @pl.when(pl.program_id(0) == 0)
    def _():
        join(cotangents, joined)

    for at in range(0, length, sub):
        spot = slice(at, at + sub)
        total = project(scalars, joined, signs_ref[spot, :], cotangents[0].shape[1]) + total_ref[:, spot]
        position = start + pl.program_id(0) * length + at + lax.broadcasted_iota(I32, (1, sub), 1)
        out_ref[:, spot] = weigh(
            total, picked_ref[:, spot], scalars, position, examples, per_shard, parties, scale
        )


def finish(scalars, cotangents, signs, picked, total, examples, start, per_shard, parties, scale):
    tokens, depth = cotangents[0].shape
    count = signs.shape[0]
    sub = CHUNK // 2
    length = count // 2 if count % (2 * sub) == 0 else count
    across = lambda i, _: (0, i)
    return pl.pallas_call(
        functools.partial(
            finish_kernel, blocks=len(cotangents), examples=examples, length=length, sub=sub, start=start,
            per_shard=per_shard, parties=parties, scale=scale,
        ),
        grid_spec=pltpu.PrefetchScalarGridSpec(
            num_scalar_prefetch=1,
            grid=(count // length,),
            in_specs=[pl.BlockSpec(piece.shape, lambda i, _: (0, 0)) for piece in cotangents]
            + [
                pl.BlockSpec((length, LANES), lambda i, _: (i, 0)),
                pl.BlockSpec((tokens, length), across),
                pl.BlockSpec((tokens, length), across),
            ],
            out_specs=pl.BlockSpec((examples, length), across),
            scratch_shapes=[pltpu.VMEM((tokens, depth * len(cotangents)), BF16)],
        ),
        out_shape=jax.ShapeDtypeStruct((examples, count), F32),
        compiler_params=pltpu.CompilerParams(vmem_limit_bytes=48 * MIB),
        cost_estimate=pl.CostEstimate(
            flops=2 * tokens * depth * len(cotangents) * count, bytes_accessed=6 * tokens * count, transcendentals=0
        ),
        name="finish_blocks",
    )(scalars, *cotangents, signs, picked, total)


def by_xor(parties, step):
    return [(source, source ^ step) for source in range(parties)]


def sum_shards(values, parties):
    step = parties // 2
    while step > 0:
        values = values + lax.ppermute(values, "param", by_xor(parties, step))
        step //= 2
    return values


def local(hidden, cotangent, sign_flips, offsets):
    examples, tokens, rows = hidden.shape
    width = sign_flips.shape[1]
    parties = lax.axis_size("param")
    own = lax.axis_index("param").astype(I32)
    per_shard = offsets.shape[0]
    count = per_shard * parties
    scale = 1.0 / math.sqrt(parties * width)
    flat = examples * tokens
    depth = cotangent.shape[2]
    held = cotangent.reshape(flat, depth)

    ringed = depth % (2 * LANES) == 0 and parties % 2 == 0
    pieces, numbers = [held], [own]
    if ringed:
        order = list(range(0, parties, 2)) + list(range(parties - 1, 0, -2))
        forward = [(order[at], order[(at + 1) % parties]) for at in range(parties)]
        backward = [(target, source) for source, target in forward]
        place = jnp.where(own % 2 == 0, own // 2, parties - 1 - own // 2)

        def shard_at(spot):
            spot = (spot + parties) % parties
            return jnp.where(spot < parties // 2, 2 * spot, 2 * (parties - spot) - 1)

        def pass_on(ahead, behind):
            return lax.ppermute(ahead, "param", forward), lax.ppermute(behind, "param", backward)

        ahead, behind = pass_on(held, held)
        arrived = []

    units = hidden.reshape(flat, rows)
    if rows % LANES:
        units = jnp.pad(units, ((0, 0), (0, -rows % LANES)))
    tile = 2 * LANES if rows % (2 * LANES) == 0 else LANES if rows % LANES == 0 else rows
    tiles = rows // tile
    table, built, step = None, 0, 1
    steps = parties.bit_length() - 1
    for at in range(steps):
        other = lax.ppermute(offsets, "param", by_xor(parties, step))
        until = -(-tiles * (at + 1) // steps)
        if until > built:
            table = build_table(sign_flips, units, table, examples, tile, (built, until - built))
            built = until
            table, other = lax.optimization_barrier((table, other))
        if ringed and at + 1 < min(steps, parties // 2):
            table, ahead, behind = lax.optimization_barrier((table, ahead, behind))
            arrived += [ahead, behind]
            ahead, behind = pass_on(ahead, behind)
        offsets = jnp.where(
            (own & step) == 0, jnp.concatenate([offsets, other]), jnp.concatenate([other, offsets])
        )
        step *= 2

    row_shift = width.bit_length() - 1
    unit_rows = (offsets >> row_shift) * (examples + SIGN_ROWS)
    line = offsets.reshape(1, count)
    eighth = count // 8
    sizes = [part * eighth for part in EARLY] if ringed else []
    sizes.append(count - sum(sizes))
    spans = [(sum(sizes[:at]), size) for at, size in enumerate(sizes)]
    sampled = []

    def scalars(first, last):
        return jnp.stack([own] + numbers[first:last])

    def sample_next(whole):
        return sample(
            scalars(0, len(pieces)), unit_rows, line, table, pieces, examples, spans[len(sampled)], width, whole,
            per_shard, parties, scale,
        )

    if ringed:
        for step in range(1, parties // 2):
            if len(arrived) < 2 * step:
                arrived += [ahead, behind]
                if step + 1 < parties // 2:
                    ahead, behind = pass_on(ahead, behind)
                else:
                    middle = flat // 2
                    ahead, behind = pass_on(ahead[:middle], behind[middle:])
            pieces += arrived[2 * step - 2:2 * step]
            numbers += [shard_at(place - step), shard_at(place + step)]
            if step > 1 and len(sampled) < len(EARLY):
                signs, picked, total = sample_next(False)
                ahead, behind, signs = lax.optimization_barrier((ahead, behind, signs))
                sampled.append((signs, picked, total, len(pieces)))
        pieces.append(jnp.concatenate([ahead, behind], axis=0))
        numbers.append(shard_at(place + parties // 2))
    else:
        gathered = lax.all_gather(cotangent, "param", axis=2, tiled=True).reshape(flat, width)
        span = 4 * LANES
        pieces = [gathered[:, at:at + span] for at in range(0, width, span)]
        numbers = [jnp.int32(at) for at in range(len(pieces))]
    whole = sample_next(True)
    parts = [whole[:, :count // 2], whole[:, count // 2:]]
    if sampled:
        parts = [
            finish(
                scalars(used, len(pieces)), pieces[used:], signs, picked, total, examples, start, per_shard, parties,
                scale,
            )
            for (signs, picked, total, used), (start, _) in zip(sampled, spans)
        ]
        parts = [jnp.concatenate(parts, axis=1), whole]
    return jnp.concatenate([sum_shards(part, parties) for part in parts], axis=1)


def solution(mesh):
    return jax.shard_map(
        local,
        mesh=mesh,
        in_specs=(
            P(("groups", "dp"), None, "param"),
            P(("groups", "dp"), None, "param"),
            P("param", None),
            P("param"),
        ),
        out_specs=P(("groups", "dp"), None),
        check_vma=False,
    )
```

```python
import functools
import math

import jax
import jax.numpy as jnp
from jax import lax
from jax.experimental import pallas as pl
from jax.experimental.pallas import tpu as pltpu
from jax.sharding import PartitionSpec as P

I32, F32, BF16 = jnp.int32, jnp.float32, jnp.bfloat16
LANES = 128
HALF = 16
SPARE = 8
SIGN_ROWS = 2
CHUNK = 512
MIB = 2**20
LAST_DIMS = (((1,), (1,)), ((), ()))


def signed(word):
    return word - 2**32 if word >= 2**31 else word


def parity(bits, count):
    shift = 1
    while shift < count:
        shift *= 2
    while shift > 1:
        shift //= 2
        bits = bits ^ (bits >> shift)
    return bits & 1


def table_kernel(flips_ref, hidden_ref, *refs, examples):
    table_ref = refs[-1]
    tile = flips_ref.shape[0]
    group = examples + SIGN_ROWS
    words = [None, None]
    for column in range(flips_ref.shape[1] // LANES):
        bit, part = column // 2, column % 2
        flips = flips_ref[:, column * LANES:(column + 1) * LANES]
        term = (flips >> 1) & 1 if bit == 0 else flips & jnp.int32(1 << bit)
        words[part] = term if words[part] is None else words[part] | term
    for part in range(2):
        table_ref[pl.ds(examples + part, tile, stride=group), :] = words[part].astype(F32)
    tokens = hidden_ref.shape[0] // examples
    for example in range(examples):
        block = hidden_ref[example * tokens:(example + 1) * tokens, :].astype(F32).T
        table_ref[pl.ds(example, tile, stride=group), :] = block[:tile]


def build_table(sign_flips, hidden, table, examples, tile, span):
    rows, width = sign_flips.shape
    first, count = span
    group = examples + SIGN_ROWS
    lanes = -(-tile // LANES) * LANES
    in_specs = [
        pl.BlockSpec((tile, width), lambda i: (i + first, 0)),
        pl.BlockSpec((hidden.shape[0], lanes), lambda i: (0, i + first)),
    ]
    args = [sign_flips, hidden]
    aliases = {}
    if table is not None:
        in_specs.append(pl.BlockSpec(memory_space=pl.ANY))
        args.append(table)
        aliases = {2: 0}
    return pl.pallas_call(
        functools.partial(table_kernel, examples=examples),
        grid=(count,),
        in_specs=in_specs,
        out_specs=pl.BlockSpec((tile * group, LANES), lambda i: (i + first, 0)),
        out_shape=jax.ShapeDtypeStruct((rows * group + SPARE, LANES), F32),
        input_output_aliases=aliases,
        compiler_params=pltpu.CompilerParams(vmem_limit_bytes=60 * MIB),
        cost_estimate=pl.CostEstimate(
            flops=2 * tile * count * width, bytes_accessed=4 * tile * count * width, transcendentals=0
        ),
        name="build_table",
    )(*args)


def hadamard_words(column):
    length = column.shape[1]
    lane = lax.broadcasted_iota(I32, (LANES, length), 0)
    words = -parity(lane & column, 7)

    def where_bit(bit, pattern):
        return -((column >> bit) & 1) & jnp.int32(signed(pattern))

    upper = where_bit(7, 0xFFFF0000)
    for bit, pattern in ((8, 0xAAAA), (9, 0xCCCC), (10, 0xF0F0), (11, 0xFF00)):
        upper = upper ^ where_bit(bit, pattern * 0x10001)
    return words ^ upper


def sign_columns(words, bits):
    pieces = []
    parts = [words.astype(jnp.int16), (words >> HALF).astype(jnp.int16)]
    for bit in bits:
        mask = jnp.int16((1 << bit) - (1 << HALF) * (bit == HALF - 1))
        for part in parts:
            pieces.append(jnp.where((part & mask) != 0, jnp.array(-1, BF16), jnp.array(1, BF16)))
    return jnp.concatenate(pieces, axis=1)


def join(scalars, cotangents, joined):
    depth = cotangents[0].shape[1]
    for at, cotangent in enumerate(cotangents):
        joined[:, pl.ds(pl.multiple_of(scalars[1 + at] * depth, depth), depth)] = cotangent[...]


def project(joined, words):
    columns = sign_columns(words, range(joined.shape[1] // (2 * LANES)))
    return lax.dot_general(joined[...], columns, LAST_DIMS, preferred_element_type=F32)


def weigh(total, picked, scalars, position, examples, per_shard, parties, scale):
    shard = position // per_shard
    sign = scale * (1 - 2 * parity(shard & scalars[0], parties.bit_length())).astype(F32)
    weighted = (total * picked.astype(F32)).reshape(examples, -1, total.shape[1])
    return jnp.sum(weighted, axis=1) * sign


def sample_kernel(
    scalars, rows_ref, offsets_ref, table_ref, *refs, blocks, examples, length, low_mask, per_shard, parties, scale
):
    cotangents, (out_ref, held, made, joined) = refs[:blocks], refs[blocks:]
    step, steps = pl.program_id(0), pl.num_programs(0)
    group = examples + SIGN_ROWS

    def copy_row(chunk, at, slot):
        row = rows_ref[chunk * length + at]
        held[slot, pl.ds(at * group, group), :] = table_ref[pl.ds(row, group), :]

    def copy_chunk(chunk):
        unroll = 32
        slot = lax.rem(chunk, 3)

        def copy_group(block, _):
            for at in range(unroll):
                copy_row(chunk, block * unroll + at, slot)
            return 0

        lax.fori_loop(0, length // unroll, copy_group, 0)

    def make_words(chunk):
        slot = lax.rem(chunk, 3)
        low, high = [held[slot, pl.ds(examples + part, length, stride=group), :].astype(I32) for part in range(2)]
        start = jnp.minimum(chunk, steps - 1) * length
        column = offsets_ref[:, pl.ds(pl.multiple_of(start, LANES), length)] & low_mask
        made[lax.rem(chunk, 2)] = (low | (high << HALF)) ^ hadamard_words(column).T

    @pl.when(step == 0)
    def _():
        join(scalars, cotangents, joined)
        copy_chunk(0)
        copy_chunk(jnp.minimum(1, steps - 1))
        make_words(0)

    words = made[lax.rem(step, 2)]
    third = jnp.minimum(step + 2, steps - 1)
    target = lax.rem(step + 2, 3)
    totals = []
    for start in range(0, length, length // 2):
        for at in range(start, start + length // 2):
            copy_row(third, at, target)
        totals.append(project(joined, words[start:start + length // 2]))
    total = jnp.concatenate(totals, axis=1)
    picked = [
        held[lax.rem(step, 3), pl.ds(example, length, stride=group), :].astype(BF16).T for example in range(examples)
    ]
    position = step * length + lax.broadcasted_iota(I32, (1, length), 1)
    out_ref[...] = weigh(
        total, jnp.concatenate(picked, axis=0), scalars, position, examples, per_shard, parties, scale
    )
    make_words(step + 1)


def sample(scalars, rows, offsets, table, cotangents, examples, width, per_shard, parties, scale):
    count = offsets.shape[1]
    tokens, depth = cotangents[0].shape
    length = CHUNK
    fixed = lambda i, *_: (0, 0)
    return pl.pallas_call(
        functools.partial(
            sample_kernel, blocks=len(cotangents), examples=examples, length=length, low_mask=width - 1,
            per_shard=per_shard, parties=parties, scale=scale,
        ),
        grid_spec=pltpu.PrefetchScalarGridSpec(
            num_scalar_prefetch=2,
            grid=(count // length,),
            in_specs=[pl.BlockSpec(offsets.shape, fixed), pl.BlockSpec(table.shape, fixed)]
            + [pl.BlockSpec(piece.shape, fixed) for piece in cotangents],
            out_specs=pl.BlockSpec((examples, length), lambda i, *_: (0, i)),
            scratch_shapes=[
                pltpu.VMEM((3, length * (examples + SIGN_ROWS) + SPARE, LANES), F32),
                pltpu.VMEM((2, length, LANES), I32),
                pltpu.VMEM((tokens, depth * len(cotangents)), BF16),
            ],
        ),
        out_shape=jax.ShapeDtypeStruct((examples, count), F32),
        compiler_params=pltpu.CompilerParams(vmem_limit_bytes=44 * MIB),
        cost_estimate=pl.CostEstimate(
            flops=2 * tokens * depth * len(cotangents) * count, bytes_accessed=6 * tokens * count, transcendentals=0
        ),
        name="sample_rows",
    )(scalars, rows, offsets, table, *cotangents)


def by_xor(parties, step):
    return [(source, source ^ step) for source in range(parties)]


def sum_shards(values, parties):
    step = parties // 2
    while step > 0:
        values = values + lax.ppermute(values, "param", by_xor(parties, step))
        step //= 2
    return values


def local(hidden, cotangent, sign_flips, offsets):
    examples, tokens, rows = hidden.shape
    width = sign_flips.shape[1]
    parties = lax.axis_size("param")
    own = lax.axis_index("param").astype(I32)
    per_shard = offsets.shape[0]
    count = per_shard * parties
    scale = 1.0 / math.sqrt(parties * width)
    flat = examples * tokens
    depth = cotangent.shape[2]
    held = cotangent.reshape(flat, depth)

    ringed = depth % (2 * LANES) == 0 and parties % 2 == 0
    pieces, numbers = [held], [own]
    if ringed:
        order = list(range(0, parties, 2)) + list(range(parties - 1, 0, -2))
        forward = [(order[at], order[(at + 1) % parties]) for at in range(parties)]
        backward = [(target, source) for source, target in forward]
        place = jnp.where(own % 2 == 0, own // 2, parties - 1 - own // 2)

        def shard_at(spot):
            spot = (spot + parties) % parties
            return jnp.where(spot < parties // 2, 2 * spot, 2 * (parties - spot) - 1)

        def pass_on(ahead, behind):
            return lax.ppermute(ahead, "param", forward), lax.ppermute(behind, "param", backward)

        ahead, behind = pass_on(held, held)
        arrived = []

    units = hidden.reshape(flat, rows)
    if rows % LANES:
        units = jnp.pad(units, ((0, 0), (0, -rows % LANES)))
    tile = 2 * LANES if rows % (2 * LANES) == 0 else LANES if rows % LANES == 0 else rows
    tiles = rows // tile
    table, built, step = None, 0, 1
    steps = parties.bit_length() - 1
    for at in range(steps):
        other = lax.ppermute(offsets, "param", by_xor(parties, step))
        until = -(-tiles * (at + 1) // steps)
        if until > built:
            table = build_table(sign_flips, units, table, examples, tile, (built, until - built))
            built = until
            table, other = lax.optimization_barrier((table, other))
        if ringed and at + 1 < min(steps, parties // 2):
            table, ahead, behind = lax.optimization_barrier((table, ahead, behind))
            arrived += [ahead, behind]
            ahead, behind = pass_on(ahead, behind)
        offsets = jnp.where(
            (own & step) == 0, jnp.concatenate([offsets, other]), jnp.concatenate([other, offsets])
        )
        step *= 2

    row_shift = width.bit_length() - 1
    unit_rows = (offsets >> row_shift) * (examples + SIGN_ROWS)
    line = offsets.reshape(1, count)
    if ringed:
        for step in range(1, parties // 2):
            if len(arrived) < 2 * step:
                arrived += [ahead, behind]
                if step + 1 < parties // 2:
                    ahead, behind = pass_on(ahead, behind)
                else:
                    middle = flat // 2
                    ahead, behind = pass_on(ahead[:middle], behind[middle:])
            pieces += arrived[2 * step - 2:2 * step]
            numbers += [shard_at(place - step), shard_at(place + step)]
        pieces.append(jnp.concatenate([ahead, behind], axis=0))
        numbers.append(shard_at(place + parties // 2))
    else:
        gathered = lax.all_gather(cotangent, "param", axis=2, tiled=True).reshape(flat, width)
        span = 4 * LANES
        pieces = [gathered[:, at:at + span] for at in range(0, width, span)]
        numbers = [jnp.int32(at) for at in range(len(pieces))]
    values = sample(
        jnp.stack([own] + numbers), unit_rows, line, table, pieces, examples, width, per_shard, parties, scale
    )
    half = count // 2
    return jnp.concatenate([sum_shards(part, parties) for part in (values[:, :half], values[:, half:])], axis=1)


def solution(mesh):
    return jax.shard_map(
        local,
        mesh=mesh,
        in_specs=(
            P(("groups", "dp"), None, "param"),
            P(("groups", "dp"), None, "param"),
            P("param", None),
            P("param"),
        ),
        out_specs=P(("groups", "dp"), None),
        check_vma=False,
    )
```

```python
import functools
import math

import jax
import jax.numpy as jnp
from jax import lax
from jax.experimental import pallas as pl
from jax.experimental.pallas import tpu as pltpu
from jax.sharding import PartitionSpec as P

I32, F32, BF16 = jnp.int32, jnp.float32, jnp.bfloat16
LANES = 128
HALF = 16
SPARE = 8
SIGN_ROWS = 2
CHUNK = 256
MIB = 2**20
LAST_DIMS = (((1,), (1,)), ((), ()))


def signed(word):
    return word - 2**32 if word >= 2**31 else word


def parity(bits, count):
    shift = 1
    while shift < count:
        shift *= 2
    while shift > 1:
        shift //= 2
        bits = bits ^ (bits >> shift)
    return bits & 1


def table_kernel(flips_ref, hidden_ref, *refs, examples):
    table_ref = refs[-1]
    tile = flips_ref.shape[0]
    group = examples + SIGN_ROWS
    words = [None, None]
    for column in range(flips_ref.shape[1] // LANES):
        bit, part = column // 2, column % 2
        flips = flips_ref[:, column * LANES:(column + 1) * LANES]
        term = (flips >> 1) & 1 if bit == 0 else flips & jnp.int32(1 << bit)
        words[part] = term if words[part] is None else words[part] | term
    for part in range(2):
        table_ref[pl.ds(examples + part, tile, stride=group), :] = words[part].astype(F32)
    tokens = hidden_ref.shape[0] // examples
    for example in range(examples):
        block = hidden_ref[example * tokens:(example + 1) * tokens, :].astype(F32).T
        table_ref[pl.ds(example, tile, stride=group), :] = block[:tile]


def build_table(sign_flips, hidden, table, examples, tile, span):
    rows, width = sign_flips.shape
    first, count = span
    group = examples + SIGN_ROWS
    lanes = -(-tile // LANES) * LANES
    in_specs = [
        pl.BlockSpec((tile, width), lambda i: (i + first, 0)),
        pl.BlockSpec((hidden.shape[0], lanes), lambda i: (0, i + first)),
    ]
    args = [sign_flips, hidden]
    aliases = {}
    if table is not None:
        in_specs.append(pl.BlockSpec(memory_space=pl.ANY))
        args.append(table)
        aliases = {2: 0}
    return pl.pallas_call(
        functools.partial(table_kernel, examples=examples),
        grid=(count,),
        in_specs=in_specs,
        out_specs=pl.BlockSpec((tile * group, LANES), lambda i: (i + first, 0)),
        out_shape=jax.ShapeDtypeStruct((rows * group + SPARE, LANES), F32),
        input_output_aliases=aliases,
        compiler_params=pltpu.CompilerParams(vmem_limit_bytes=60 * MIB),
        cost_estimate=pl.CostEstimate(
            flops=2 * tile * count * width, bytes_accessed=4 * tile * count * width, transcendentals=0
        ),
        name="build_table",
    )(*args)


def hadamard_words(column):
    length = column.shape[1]
    lane = lax.broadcasted_iota(I32, (LANES, length), 0)
    words = -parity(lane & column, 7)

    def where_bit(bit, pattern):
        return -((column >> bit) & 1) & jnp.int32(signed(pattern))

    upper = where_bit(7, 0xFFFF0000)
    for bit, pattern in ((8, 0xAAAA), (9, 0xCCCC), (10, 0xF0F0), (11, 0xFF00)):
        upper = upper ^ where_bit(bit, pattern * 0x10001)
    return words ^ upper


def sign_columns(words, bits):
    pieces = []
    parts = [words.astype(jnp.int16), (words >> HALF).astype(jnp.int16)]
    for bit in bits:
        mask = jnp.int16((1 << bit) - (1 << HALF) * (bit == HALF - 1))
        for part in parts:
            pieces.append(jnp.where((part & mask) != 0, jnp.array(-1, BF16), jnp.array(1, BF16)))
    return jnp.concatenate(pieces, axis=1)


def join(scalars, cotangents, joined):
    depth = cotangents[0].shape[1]
    for at, cotangent in enumerate(cotangents):
        joined[:, pl.ds(pl.multiple_of(scalars[1 + at] * depth, depth), depth)] = cotangent[...]


def project(joined, words):
    columns = sign_columns(words, range(joined.shape[1] // (2 * LANES)))
    return lax.dot_general(joined[...], columns, LAST_DIMS, preferred_element_type=F32)


def weigh(total, picked, scalars, position, examples, per_shard, parties, scale):
    shard = position // per_shard
    sign = scale * (1 - 2 * parity(shard & scalars[0], parties.bit_length())).astype(F32)
    weighted = (total * picked.astype(F32)).reshape(examples, -1, total.shape[1])
    return jnp.sum(weighted, axis=1) * sign


def sample_kernel(
    scalars, rows_ref, offsets_ref, table_ref, *refs, blocks, examples, length, low_mask, per_shard, parties, scale
):
    cotangents, (out_ref, held, made, joined) = refs[:blocks], refs[blocks:]
    step, steps = pl.program_id(0), pl.num_programs(0)
    group = examples + SIGN_ROWS

    def copy_row(chunk, at, slot):
        row = rows_ref[chunk * length + at]
        held[slot, pl.ds(at * group, group), :] = table_ref[pl.ds(row, group), :]

    def copy_chunk(chunk):
        unroll = 32
        slot = lax.rem(chunk, 3)

        def copy_group(block, _):
            for at in range(unroll):
                copy_row(chunk, block * unroll + at, slot)
            return 0

        lax.fori_loop(0, length // unroll, copy_group, 0)

    def make_words(chunk):
        slot = lax.rem(chunk, 3)
        low, high = [held[slot, pl.ds(examples + part, length, stride=group), :].astype(I32) for part in range(2)]
        start = jnp.minimum(chunk, steps - 1) * length
        column = offsets_ref[:, pl.ds(pl.multiple_of(start, LANES), length)] & low_mask
        made[lax.rem(chunk, 2)] = (low | (high << HALF)) ^ hadamard_words(column).T

    @pl.when(step == 0)
    def _():
        join(scalars, cotangents, joined)
        copy_chunk(0)
        copy_chunk(jnp.minimum(1, steps - 1))
        make_words(0)

    words = made[lax.rem(step, 2)]
    third = jnp.minimum(step + 2, steps - 1)
    target = lax.rem(step + 2, 3)
    for at in range(length):
        copy_row(third, at, target)
    total = project(joined, words)
    picked = [
        held[lax.rem(step, 3), pl.ds(example, length, stride=group), :].astype(BF16).T for example in range(examples)
    ]
    position = step * length + lax.broadcasted_iota(I32, (1, length), 1)
    out_ref[...] = weigh(
        total, jnp.concatenate(picked, axis=0), scalars, position, examples, per_shard, parties, scale
    )
    make_words(step + 1)


def sample(scalars, rows, offsets, table, cotangents, examples, width, per_shard, parties, scale):
    count = offsets.shape[1]
    tokens, depth = cotangents[0].shape
    length = CHUNK
    fixed = lambda i, *_: (0, 0)
    return pl.pallas_call(
        functools.partial(
            sample_kernel, blocks=len(cotangents), examples=examples, length=length, low_mask=width - 1,
            per_shard=per_shard, parties=parties, scale=scale,
        ),
        grid_spec=pltpu.PrefetchScalarGridSpec(
            num_scalar_prefetch=2,
            grid=(count // length,),
            in_specs=[pl.BlockSpec(offsets.shape, fixed), pl.BlockSpec(table.shape, fixed)]
            + [pl.BlockSpec(piece.shape, fixed) for piece in cotangents],
            out_specs=pl.BlockSpec((examples, length), lambda i, *_: (0, i)),
            scratch_shapes=[
                pltpu.VMEM((3, length * (examples + SIGN_ROWS) + SPARE, LANES), F32),
                pltpu.VMEM((2, length, LANES), I32),
                pltpu.VMEM((tokens, depth * len(cotangents)), BF16),
            ],
        ),
        out_shape=jax.ShapeDtypeStruct((examples, count), F32),
        compiler_params=pltpu.CompilerParams(vmem_limit_bytes=44 * MIB),
        cost_estimate=pl.CostEstimate(
            flops=2 * tokens * depth * len(cotangents) * count, bytes_accessed=6 * tokens * count, transcendentals=0
        ),
        name="sample_rows",
    )(scalars, rows, offsets, table, *cotangents)


def by_xor(parties, step):
    return [(source, source ^ step) for source in range(parties)]


def sum_shards(values, parties):
    step = parties // 2
    while step > 0:
        values = values + lax.ppermute(values, "param", by_xor(parties, step))
        step //= 2
    return values


def local(hidden, cotangent, sign_flips, offsets):
    examples, tokens, rows = hidden.shape
    width = sign_flips.shape[1]
    parties = lax.axis_size("param")
    own = lax.axis_index("param").astype(I32)
    per_shard = offsets.shape[0]
    count = per_shard * parties
    scale = 1.0 / math.sqrt(parties * width)
    flat = examples * tokens
    depth = cotangent.shape[2]
    held = cotangent.reshape(flat, depth)

    ringed = depth % (2 * LANES) == 0 and parties % 2 == 0
    pieces, numbers = [held], [own]
    if ringed:
        order = list(range(0, parties, 2)) + list(range(parties - 1, 0, -2))
        forward = [(order[at], order[(at + 1) % parties]) for at in range(parties)]
        backward = [(target, source) for source, target in forward]
        place = jnp.where(own % 2 == 0, own // 2, parties - 1 - own // 2)

        def shard_at(spot):
            spot = (spot + parties) % parties
            return jnp.where(spot < parties // 2, 2 * spot, 2 * (parties - spot) - 1)

        def pass_on(ahead, behind):
            return lax.ppermute(ahead, "param", forward), lax.ppermute(behind, "param", backward)

        ahead, behind = pass_on(held, held)
        arrived = []

    units = hidden.reshape(flat, rows)
    if rows % LANES:
        units = jnp.pad(units, ((0, 0), (0, -rows % LANES)))
    tile = 2 * LANES if rows % (2 * LANES) == 0 else LANES if rows % LANES == 0 else rows
    tiles = rows // tile
    table, built, step = None, 0, 1
    steps = parties.bit_length() - 1
    for at in range(steps):
        other = lax.ppermute(offsets, "param", by_xor(parties, step))
        until = -(-tiles * (at + 1) // steps)
        if until > built:
            table = build_table(sign_flips, units, table, examples, tile, (built, until - built))
            built = until
            table, other = lax.optimization_barrier((table, other))
        if ringed and at + 1 < min(steps, parties // 2):
            table, ahead, behind = lax.optimization_barrier((table, ahead, behind))
            arrived += [ahead, behind]
            ahead, behind = pass_on(ahead, behind)
        offsets = jnp.where(
            (own & step) == 0, jnp.concatenate([offsets, other]), jnp.concatenate([other, offsets])
        )
        step *= 2

    row_shift = width.bit_length() - 1
    unit_rows = (offsets >> row_shift) * (examples + SIGN_ROWS)
    line = offsets.reshape(1, count)
    if ringed:
        for step in range(1, parties // 2):
            if len(arrived) < 2 * step:
                arrived += [ahead, behind]
                if step + 1 < parties // 2:
                    ahead, behind = pass_on(ahead, behind)
                else:
                    middle = flat // 2
                    ahead, behind = pass_on(ahead[:middle], behind[middle:])
            pieces += arrived[2 * step - 2:2 * step]
            numbers += [shard_at(place - step), shard_at(place + step)]
        pieces.append(jnp.concatenate([ahead, behind], axis=0))
        numbers.append(shard_at(place + parties // 2))
    else:
        gathered = lax.all_gather(cotangent, "param", axis=2, tiled=True).reshape(flat, width)
        span = 4 * LANES
        pieces = [gathered[:, at:at + span] for at in range(0, width, span)]
        numbers = [jnp.int32(at) for at in range(len(pieces))]
    values = sample(
        jnp.stack([own] + numbers), unit_rows, line, table, pieces, examples, width, per_shard, parties, scale
    )
    half = count // 2
    return jnp.concatenate([sum_shards(part, parties) for part in (values[:, :half], values[:, half:])], axis=1)


def solution(mesh):
    return jax.shard_map(
        local,
        mesh=mesh,
        in_specs=(
            P(("groups", "dp"), None, "param"),
            P(("groups", "dp"), None, "param"),
            P("param", None),
            P("param"),
        ),
        out_specs=P(("groups", "dp"), None),
        check_vma=False,
    )
```

```python
import functools
import math

import jax
import jax.numpy as jnp
from jax import lax
from jax.experimental import pallas as pl
from jax.experimental.pallas import tpu as pltpu
from jax.sharding import PartitionSpec as P

I32, F32, BF16 = jnp.int32, jnp.float32, jnp.bfloat16
LANES = 128
HALF = 16
SPARE = 8
SIGN_ROWS = 2
CHUNK = 256
MIB = 2**20
LAST_DIMS = (((1,), (1,)), ((), ()))


def signed(word):
    return word - 2**32 if word >= 2**31 else word


def parity(bits, count):
    shift = 1
    while shift < count:
        shift *= 2
    while shift > 1:
        shift //= 2
        bits = bits ^ (bits >> shift)
    return bits & 1


def table_kernel(flips_ref, hidden_ref, *refs, examples):
    table_ref = refs[-1]
    tile = flips_ref.shape[0]
    group = examples + SIGN_ROWS
    words = [None, None]
    for column in range(flips_ref.shape[1] // LANES):
        bit, part = column // 2, column % 2
        flips = flips_ref[:, column * LANES:(column + 1) * LANES]
        term = (flips >> 1) & 1 if bit == 0 else flips & jnp.int32(1 << bit)
        words[part] = term if words[part] is None else words[part] | term
    for part in range(2):
        table_ref[pl.ds(examples + part, tile, stride=group), :] = words[part].astype(F32)
    tokens = hidden_ref.shape[0] // examples
    for example in range(examples):
        block = hidden_ref[example * tokens:(example + 1) * tokens, :].astype(F32).T
        table_ref[pl.ds(example, tile, stride=group), :] = block[:tile]


def build_table(sign_flips, hidden, table, examples, tile, span):
    rows, width = sign_flips.shape
    first, count = span
    group = examples + SIGN_ROWS
    lanes = -(-tile // LANES) * LANES
    in_specs = [
        pl.BlockSpec((tile, width), lambda i: (i + first, 0)),
        pl.BlockSpec((hidden.shape[0], lanes), lambda i: (0, i + first)),
    ]
    args = [sign_flips, hidden]
    aliases = {}
    if table is not None:
        in_specs.append(pl.BlockSpec(memory_space=pl.ANY))
        args.append(table)
        aliases = {2: 0}
    return pl.pallas_call(
        functools.partial(table_kernel, examples=examples),
        grid=(count,),
        in_specs=in_specs,
        out_specs=pl.BlockSpec((tile * group, LANES), lambda i: (i + first, 0)),
        out_shape=jax.ShapeDtypeStruct((rows * group + SPARE, LANES), F32),
        input_output_aliases=aliases,
        compiler_params=pltpu.CompilerParams(vmem_limit_bytes=60 * MIB),
        cost_estimate=pl.CostEstimate(
            flops=2 * tile * count * width, bytes_accessed=4 * tile * count * width, transcendentals=0
        ),
        name="build_table",
    )(*args)


def hadamard_words(column):
    length = column.shape[1]
    lane = lax.broadcasted_iota(I32, (LANES, length), 0)
    words = -parity(lane & column, 7)

    def where_bit(bit, pattern):
        return -((column >> bit) & 1) & jnp.int32(signed(pattern))

    upper = where_bit(7, 0xFFFF0000)
    for bit, pattern in ((8, 0xAAAA), (9, 0xCCCC), (10, 0xF0F0), (11, 0xFF00)):
        upper = upper ^ where_bit(bit, pattern * 0x10001)
    return words ^ upper


def sign_columns(words, bits):
    pieces = []
    parts = [words.astype(jnp.int16), (words >> HALF).astype(jnp.int16)]
    for bit in bits:
        mask = jnp.int16((1 << bit) - (1 << HALF) * (bit == HALF - 1))
        for part in parts:
            pieces.append(jnp.where((part & mask) != 0, jnp.array(-1, BF16), jnp.array(1, BF16)))
    return jnp.concatenate(pieces, axis=1)


def join(scalars, cotangents, joined):
    depth = cotangents[0].shape[1]
    for at, cotangent in enumerate(cotangents):
        joined[:, pl.ds(pl.multiple_of(scalars[1 + at] * depth, depth), depth)] = cotangent[...]


def project(joined, words):
    columns = sign_columns(words, range(joined.shape[1] // (2 * LANES)))
    return lax.dot_general(joined[...], columns, LAST_DIMS, preferred_element_type=F32)


def weigh(total, picked, scalars, position, examples, per_shard, parties, scale):
    shard = position // per_shard
    sign = scale * (1 - 2 * parity(shard & scalars[0], parties.bit_length())).astype(F32)
    weighted = (total * picked.astype(F32)).reshape(examples, -1, total.shape[1])
    return jnp.sum(weighted, axis=1) * sign


def sample_kernel(
    scalars, rows_ref, offsets_ref, table_ref, *refs, blocks, examples, length, low_mask, per_shard, parties, scale
):
    cotangents, (out_ref, held, made, joined) = refs[:blocks], refs[blocks:]
    step, steps = pl.program_id(0), pl.num_programs(0)
    group = examples + SIGN_ROWS

    def copy_row(chunk, at, slot):
        row = rows_ref[chunk * length + at]
        held[slot, pl.ds(at * group, group), :] = table_ref[pl.ds(row, group), :]

    def copy_chunk(chunk):
        unroll = 32
        slot = lax.rem(chunk, 3)

        def copy_group(block, _):
            for at in range(unroll):
                copy_row(chunk, block * unroll + at, slot)
            return 0

        lax.fori_loop(0, length // unroll, copy_group, 0)

    def make_words(chunk):
        slot = lax.rem(chunk, 3)
        low, high = [held[slot, pl.ds(examples + part, length, stride=group), :].astype(I32) for part in range(2)]
        start = jnp.minimum(chunk, steps - 1) * length
        column = offsets_ref[:, pl.ds(pl.multiple_of(start, LANES), length)] & low_mask
        made[lax.rem(chunk, 2)] = (low | (high << HALF)) ^ hadamard_words(column).T

    @pl.when(step == 0)
    def _():
        join(scalars, cotangents, joined)
        copy_chunk(0)
        copy_chunk(jnp.minimum(1, steps - 1))
        make_words(0)

    words = made[lax.rem(step, 2)]
    third = jnp.minimum(step + 2, steps - 1)
    target = lax.rem(step + 2, 3)
    for at in range(length):
        copy_row(third, at, target)
    total = project(joined, words)
    picked = [
        held[lax.rem(step, 3), pl.ds(example, length, stride=group), :].astype(BF16).T for example in range(examples)
    ]
    position = step * length + lax.broadcasted_iota(I32, (1, length), 1)
    out_ref[...] = weigh(
        total, jnp.concatenate(picked, axis=0), scalars, position, examples, per_shard, parties, scale
    )
    make_words(step + 1)


def sample(scalars, rows, offsets, table, cotangents, examples, width, per_shard, parties, scale):
    count = offsets.shape[1]
    tokens, depth = cotangents[0].shape
    length = CHUNK
    fixed = lambda i, *_: (0, 0)
    return pl.pallas_call(
        functools.partial(
            sample_kernel, blocks=len(cotangents), examples=examples, length=length, low_mask=width - 1,
            per_shard=per_shard, parties=parties, scale=scale,
        ),
        grid_spec=pltpu.PrefetchScalarGridSpec(
            num_scalar_prefetch=2,
            grid=(count // length,),
            in_specs=[pl.BlockSpec(offsets.shape, fixed), pl.BlockSpec(table.shape, fixed)]
            + [pl.BlockSpec(piece.shape, fixed) for piece in cotangents],
            out_specs=pl.BlockSpec((examples, length), lambda i, *_: (0, i)),
            scratch_shapes=[
                pltpu.VMEM((3, length * (examples + SIGN_ROWS) + SPARE, LANES), F32),
                pltpu.VMEM((2, length, LANES), I32),
                pltpu.VMEM((tokens, depth * len(cotangents)), BF16),
            ],
        ),
        out_shape=jax.ShapeDtypeStruct((examples, count), F32),
        compiler_params=pltpu.CompilerParams(vmem_limit_bytes=44 * MIB),
        cost_estimate=pl.CostEstimate(
            flops=2 * tokens * depth * len(cotangents) * count, bytes_accessed=6 * tokens * count, transcendentals=0
        ),
        name="sample_rows",
    )(scalars, rows, offsets, table, *cotangents)


def by_xor(parties, step):
    return [(source, source ^ step) for source in range(parties)]


def sum_shards(values, parties, turn):
    steps = [parties >> (at + 1) for at in range(parties.bit_length() - 1)]
    for step in steps[turn:] + steps[:turn]:
        values = values + lax.ppermute(values, "param", by_xor(parties, step))
    return values


def local(hidden, cotangent, sign_flips, offsets):
    examples, tokens, rows = hidden.shape
    width = sign_flips.shape[1]
    parties = lax.axis_size("param")
    own = lax.axis_index("param").astype(I32)
    per_shard = offsets.shape[0]
    count = per_shard * parties
    scale = 1.0 / math.sqrt(parties * width)
    flat = examples * tokens
    depth = cotangent.shape[2]
    held = cotangent.reshape(flat, depth)

    ringed = depth % (2 * LANES) == 0 and parties % 2 == 0
    pieces, numbers = [held], [own]
    if ringed:
        order = list(range(0, parties, 2)) + list(range(parties - 1, 0, -2))
        forward = [(order[at], order[(at + 1) % parties]) for at in range(parties)]
        backward = [(target, source) for source, target in forward]
        place = jnp.where(own % 2 == 0, own // 2, parties - 1 - own // 2)

        def shard_at(spot):
            spot = (spot + parties) % parties
            return jnp.where(spot < parties // 2, 2 * spot, 2 * (parties - spot) - 1)

        def pass_on(ahead, behind):
            return lax.ppermute(ahead, "param", forward), lax.ppermute(behind, "param", backward)

        ahead, behind = pass_on(held, held)
        arrived = []

    units = hidden.reshape(flat, rows)
    if rows % LANES:
        units = jnp.pad(units, ((0, 0), (0, -rows % LANES)))
    tile = 2 * LANES if rows % (2 * LANES) == 0 else LANES if rows % LANES == 0 else rows
    tiles = rows // tile
    table, built, step = None, 0, 1
    steps = parties.bit_length() - 1
    for at in range(steps):
        other = lax.ppermute(offsets, "param", by_xor(parties, step))
        until = -(-tiles * (at + 1) // steps)
        if until > built:
            table = build_table(sign_flips, units, table, examples, tile, (built, until - built))
            built = until
            table, other = lax.optimization_barrier((table, other))
        if ringed and at + 1 < min(steps, parties // 2):
            table, ahead, behind = lax.optimization_barrier((table, ahead, behind))
            arrived += [ahead, behind]
            ahead, behind = pass_on(ahead, behind)
        offsets = jnp.where(
            (own & step) == 0, jnp.concatenate([offsets, other]), jnp.concatenate([other, offsets])
        )
        step *= 2

    row_shift = width.bit_length() - 1
    unit_rows = (offsets >> row_shift) * (examples + SIGN_ROWS)
    line = offsets.reshape(1, count)
    if ringed:
        for step in range(1, parties // 2):
            if len(arrived) < 2 * step:
                arrived += [ahead, behind]
                if step + 1 < parties // 2:
                    ahead, behind = pass_on(ahead, behind)
                else:
                    middle = flat // 2
                    ahead, behind = pass_on(ahead[:middle], behind[middle:])
            pieces += arrived[2 * step - 2:2 * step]
            numbers += [shard_at(place - step), shard_at(place + step)]
        pieces.append(jnp.concatenate([ahead, behind], axis=0))
        numbers.append(shard_at(place + parties // 2))
    else:
        gathered = lax.all_gather(cotangent, "param", axis=2, tiled=True).reshape(flat, width)
        span = 4 * LANES
        pieces = [gathered[:, at:at + span] for at in range(0, width, span)]
        numbers = [jnp.int32(at) for at in range(len(pieces))]
    values = sample(
        jnp.stack([own] + numbers), unit_rows, line, table, pieces, examples, width, per_shard, parties, scale
    )
    half = count // 2
    parts = [sum_shards(part, parties, turn) for turn, part in enumerate((values[:, :half], values[:, half:]))]
    return jnp.concatenate(parts, axis=1)


def solution(mesh):
    return jax.shard_map(
        local,
        mesh=mesh,
        in_specs=(
            P(("groups", "dp"), None, "param"),
            P(("groups", "dp"), None, "param"),
            P("param", None),
            P("param"),
        ),
        out_specs=P(("groups", "dp"), None),
        check_vma=False,
    )
```
